512 devices in a mesh: depth: 8 (over z), tx: 8 (over y_hi, core), ty: 8 (over x, y_lo).
Axes of the slice: x: 4, y: 8 (y_hi: 4, y_lo: 2; y = y_hi * 2 + y_lo), z: 8, core: 2. Of those that a mesh axis runs over, the one named last changes fastest.
Arguments:
- mask: int32 [8, 512, 4096], P('tx', 'depth', 'ty'), may hold values from 0 to 1, as said below
- kernels: bfloat16 [8, 12, 64, 128], P('depth'), may hold values from -6 to 6
- weights: float32 [12], replicated, may hold values from 0.02 to 0.2
- band_rows: int32 [64], replicated, may hold values from 0 to 127, as said below
- band_cols: int32 [64], replicated, may hold values from 0 to 127, as said below
- quencher: float32 [8, 8, 512, 4096], P(None, 'tx', 'depth', 'ty'), may hold values from 0.1 to 0.6
Outputs:
- acid: float32 [8, 8, 512, 4096], P(None, 'tx', 'depth', 'ty')
- quencher_left: float32 [8, 8, 512, 4096], P(None, 'tx', 'depth', 'ty')
The draws below stay inside these ranges and needn't reach their ends.
Inputs may be any that keep to these rules, and one draw needn't show every extreme that they name: `mask`: 0 or 1, equal on each aligned block of 2 x 2 pixels. `band_rows`: 64 distinct band indices. `band_cols`: 64 distinct band indices.
All inputs are finite; a program needn't handle non-finite values.
Results may differ from the reference program's by a relative error of at most 0.0016.
Values may be sent and summed in bfloat16 or wider, within the bound.
No kernel may reach another device: no remote copies, remote signals or barrier semaphores. Data moves between devices by JAX's collectives and lax.ppermute only.
A program may use at most 64 MiB of HBM per device.

```python
import math
import jax
import jax.numpy as jnp
from jax import lax

TILE = 512
BAND = 64
KERN = 12
STEPS = 2
DEPTHS = 8
TILES_X = 8
NY = 4096
N_TX = 8
N_TY = 8


def draw_mask(key, part):
    key = jax.random.fold_in(key, 11)
    coarse = jax.random.randint(key, (TILES_X, TILE // 2, NY // 2), 0, 2, dtype=jnp.int32)
    return jnp.repeat(jnp.repeat(coarse, 2, axis=1), 2, axis=2)


def pick_band(key):
    key_inner, key_order = jax.random.split(key)
    interior = jax.random.permutation(key_inner, 2 * BAND - 2)[:BAND - 2].astype(jnp.int32) + 1
    extremes = jnp.array([0, 2 * BAND - 1], jnp.int32)
    return jax.random.permutation(key_order, jnp.concatenate([extremes, interior], 0)).astype(jnp.int32)


def draw_band_rows(key, part):
    key = jax.random.fold_in(key, 21)
    return pick_band(key)


def draw_band_cols(key, part):
    key = jax.random.fold_in(key, 23)
    return pick_band(key)


def steps_of(own_key, shape, pieces, smallest, top_value):
    factor_of, own = 1.0, jax.random.fold_in(own_key, 6)
    for dim, parts in pieces:
        steps = jnp.exp(jax.random.uniform(jax.random.fold_in(own, dim), (parts,), jnp.float32, smallest / len(pieces), top_value / len(pieces)))
        factor_of = factor_of * jnp.repeat(steps, shape[dim] // parts).reshape([-1 if axis == dim else 1 for axis in range(len(shape))])
    return factor_of


def centred(own_key, extent, deviation, most, shards=(), kind=jnp.bfloat16):
    level = steps_of(own_key, extent, shards, -0.22, 0.18) if shards else 1.0
    entries = jax.random.normal(own_key, extent, jnp.float32) * deviation * level
    return jnp.minimum(jnp.maximum(entries, -most), most).astype(kind)


def setup_inputs(seed: int = 0) -> dict:
    seeds = jax.random.split(jax.random.key(seed), 7)
    return {
        "mask": draw_mask(jax.random.fold_in(seeds[6], 71), 0),
        "kernels": centred(seeds[1], (DEPTHS, KERN, BAND, 2 * BAND), 1.0, 6.0, ((0, 8),)),
        "weights": jnp.clip(jnp.exp(jax.random.uniform(seeds[2], (KERN,), jnp.float32, math.log(0.02), math.log(0.2))), 0.02, 0.2),
        "band_rows": draw_band_rows(jax.random.fold_in(seeds[6], 71), 0),
        "band_cols": draw_band_cols(jax.random.fold_in(seeds[6], 71), 0),
        "quencher": jnp.clip(0.1 + 0.5 * jax.random.uniform(seeds[5], (DEPTHS, TILES_X, TILE, NY), jnp.float32) ** steps_of(seeds[5], (DEPTHS, TILES_X, TILE, NY), ((1, 8), (2, 8), (3, 8)), -0.2, 0.2), 0.1, 0.6),
    }


DILL_RATE = 1.0
REACT_RATE = 0.4


def phase_table(freqs, length, offset, count):
    coords = offset + jnp.arange(count, dtype=jnp.int32)
    index = jnp.mod(coords[:, None] * freqs[None, :], length)
    angle = index.astype(jnp.float32) * (2.0 * math.pi / length)
    return jnp.cos(angle), jnp.sin(angle)


def mask_spectrum(rows, cos_x, sin_x, cos_y, sin_y):
    band = cos_y.shape[1]
    highest = lax.Precision.HIGHEST
    summed = jnp.dot(rows, jnp.concatenate([cos_y, sin_y], 1), precision=highest)
    first = jnp.dot(cos_x.T, summed, precision=highest)
    second = jnp.dot(sin_x.T, summed, precision=highest)
    real = first[:, :band] - second[:, band:]
    imag = -(second[:, :band] + first[:, band:])
    return real, imag


def column_block(cos_y, sin_y):
    upper = jnp.concatenate([cos_y.T, sin_y.T], 1)
    lower = jnp.concatenate([-sin_y.T, cos_y.T], 1)
    return jnp.concatenate([upper, lower], 0).astype(jnp.bfloat16)


def plane_intensity(kernel, weights, spec_re, spec_im, row_table, col_table):
    band = spec_re.shape[0]
    height = row_table.shape[0]
    width = col_table.shape[1] // 2

    def add_kernel(index, total):
        current = kernel[index].astype(jnp.float32)
        k_re = current[:, :band]
        k_im = current[:, band:]
        s_re = (k_re * spec_re - k_im * spec_im).astype(jnp.bfloat16)
        s_im = (k_re * spec_im + k_im * spec_re).astype(jnp.bfloat16)
        block = jnp.concatenate([jnp.concatenate([s_re, s_im], 1), jnp.concatenate([-s_im, s_re], 1)], 0)
        half = jnp.dot(row_table, block, preferred_element_type=jnp.float32).astype(jnp.bfloat16)
        field = jnp.dot(half, col_table, preferred_element_type=jnp.float32)
        power = field[:, :width] * field[:, :width] + field[:, width:] * field[:, width:]
        return total + weights[index] * power

    return lax.fori_loop(0, kernel.shape[0], add_kernel, jnp.zeros((height, width), jnp.float32))


def lateral_sum(field):
    return (jnp.roll(field, 1, 1) + jnp.roll(field, -1, 1) + jnp.roll(field, 1, 2)
            + jnp.roll(field, -1, 2) - 4.0 * field)


def vertical_sum(field):
    above = jnp.concatenate([field[1:], field[-1:]], 0)
    below = jnp.concatenate([field[:1], field[:-1]], 0)
    return above + below - 2.0 * field


def reference(mask, kernels, weights, band_rows, band_cols, quencher):
    freq_x = band_rows - BAND // 2
    freq_y = band_cols - BAND // 2
    cos_x, sin_x = phase_table(freq_x, TILE, 0, TILE)
    cos_y, sin_y = phase_table(freq_y, TILE, 0, TILE)
    row_table = jnp.concatenate([cos_x, sin_x], 1).astype(jnp.bfloat16)
    col_table = column_block(cos_y, sin_y)
    scale = 1.0 / (TILE * TILE)
    tiles = mask.reshape(N_TX, TILE, N_TY, TILE).transpose(0, 2, 1, 3).reshape(N_TX * N_TY, TILE, TILE)

    def image_tile(pixels):
        spec_re, spec_im = mask_spectrum(pixels.astype(jnp.float32), cos_x, sin_x, cos_y, sin_y)
        spec_re = spec_re * scale
        spec_im = spec_im * scale
        planes = [plane_intensity(kernels[plane], weights, spec_re, spec_im, row_table, col_table)
                  for plane in range(DEPTHS)]
        return jnp.stack(planes, 0)

    images = lax.map(image_tile, tiles)
    intensity = images.reshape(N_TX, N_TY, DEPTHS, TILE, TILE).transpose(2, 0, 3, 1, 4)
    intensity = intensity.reshape(DEPTHS, N_TX * TILE, N_TY * TILE)
    acid = 1.0 - jnp.exp(-DILL_RATE * intensity)
    base = quencher.reshape(DEPTHS, N_TX * TILE, N_TY * TILE)
    for turn in range(STEPS):
        react = REACT_RATE * acid * base
        acid_next = acid + 0.23 * lateral_sum(acid) + 0.03 * vertical_sum(acid) - react
        base = base + 0.15 * lateral_sum(base) + 0.05 * vertical_sum(base) - react
        acid = acid_next
    shape = (DEPTHS, N_TX, TILE, N_TY * TILE)
    return acid.reshape(shape), base.reshape(shape)
```

```python
import functools
import math

import jax
import jax.numpy as jnp
import numpy as np
from jax import lax
from jax.experimental import pallas as pl
from jax.experimental.pallas import tpu as pltpu
from jax.sharding import PartitionSpec as P

BF = jnp.bfloat16
F32 = jnp.float32
TILE = 512
BAND = 64
HALF = 256
PLANES = 8
STRIP = 64
CYC = 72
WIDE = 640
DILL_RATE = 1.0
REACT_RATE = 0.4
ACID_LAT, ACID_VERT = 0.23, 0.03
QUEN_LAT, QUEN_VERT = 0.15, 0.05
VMEM = pl.BlockSpec(memory_space=pltpu.VMEM)
SMEM = pl.BlockSpec(memory_space=pltpu.SMEM)
LIMIT = 40 * 1024 * 1024
MOST = 60 * 1024 * 1024


def split(x):
    hi = np.asarray(x, np.float32).astype(jnp.bfloat16)
    lo = (np.asarray(x, np.float64) - hi.astype(np.float64)).astype(np.float32).astype(jnp.bfloat16)
    return hi, lo


@functools.cache
def constants():
    u = np.arange(TILE)
    f = np.arange(128) - BAND // 2
    angle = np.mod(u[:, None] * f[None, :], TILE) * (2.0 * np.pi / TILE)
    cs = np.concatenate([np.cos(angle), np.sin(angle)], 1)
    n = np.arange(HALF)
    m = np.arange(1, 128)
    gap = np.mod(u[None, :] - 2 * n[:, None], TILE)
    line = (1.0 + 2.0 * np.cos(2.0 * np.pi * m[None, :] * u[:, None] / TILE).sum(1)) / HALF
    spread = line[gap]
    spread[:, 0::2] = np.eye(HALF)
    out = {}
    out["cs"] = split(cs)[0]
    out["pairs_hi"], out["pairs_lo"] = split(cs[0::2] + cs[1::2])
    out["even_t"] = split(cs[0::2].T)[0]
    edge = np.zeros((16, 256))
    edge[:4] = cs[[0, 1, TILE - 2, TILE - 1]]
    out["edge"] = split(edge)[0]
    out["spread"] = np.concatenate(split(spread), 0)
    return out


def dot(a, b):
    return lax.dot_general(a, b, (((1,), (0,)), ((), ())), preferred_element_type=F32)


def dot_nt(a, b):
    return lax.dot_general(a, b, (((1,), (1,)), ((), ())), preferred_element_type=F32)


def dot_tn(a, b):
    return lax.dot_general(a, b, (((0,), (0,)), ((), ())), preferred_element_type=F32)


def iota(shape, dim):
    return lax.broadcasted_iota(jnp.int32, shape, dim)


def fetch(sem, *pairs):
    copies = [pltpu.make_async_copy(src, dst, sem.at[i]) for i, (src, dst) in enumerate(pairs)]
    for copy in copies:
        copy.start()
    return copies


def picker(band_ref):
    band = band_ref[...]
    return (iota((256, 128), 0) == jnp.concatenate([band, band + 128], 1)).astype(BF)


def columns():
    row = iota((16, TILE), 0)
    col = jnp.where(row < 2, row, row + TILE - 4)
    return ((iota((16, TILE), 1) == col) & (row < 4)).astype(BF)


def strip_kernel(mask_in, quen_in, out_ref, mask, head, tail, edge, sem):
    copies = fetch(
        sem, *[(mask_in.at[:, pl.ds(128 * c, 128)], mask.at[c]) for c in range(4)],
        (quen_in.at[:, pl.ds(0, 8), :], head), (quen_in.at[:, pl.ds(STRIP - 8, 8), :], tail),
    )
    halves = (iota((TILE, HALF), 0) == 2 * iota((TILE, HALF), 1)).astype(BF)
    before = lax.rem(lax.axis_index("depth") + 7, 8)
    for copy in copies[:4]:
        copy.wait()
    rows = [mask[c, pl.ds(0, STRIP // 2, stride=2), :] for c in range(4)]
    coarse = dot(jnp.concatenate(rows, 1).astype(F32).astype(BF), halves).astype(BF)
    for copy in copies[4:]:
        copy.wait()
    for z in range(PLANES):
        for r in range(2):
            edge[8 * r + z : 8 * r + z + 1, :] = head[z, r : r + 1, :]
            edge[16 + 8 * r + z : 17 + 8 * r + z, :] = tail[z, 6 + r : 7 + r, :]
    top = edge[0:16].astype(BF)
    bottom = edge[16:32].astype(BF)
    for peer in range(8):
        out_ref[peer, 0:32, :] = coarse[:, 0:128]
        out_ref[peer, 32:64, :] = coarse[:, 128:256]
        ours = jnp.where(before == peer, top, bottom)
        for c in range(4):
            out_ref[peer, 64 + 16 * c : 80 + 16 * c, :] = ours[:, 128 * c : 128 * (c + 1)]


def table_kernel(
    after, bx_in, by_in, cs_in, hi_in, lo_in, even_in, edge_in, quen_in, w_in,
    rows_ref, xhi_ref, xlo_ref, yhi_ref, ylo_ref, cols_ref, placed_ref, side_ref, weight_ref,
    bx, by, cs, hi_tab, lo_tab, even, edge, quen, w, sem,
):
    copies = fetch(
        sem, (bx_in, bx), (by_in, by), (edge_in, edge), (even_in, even), (cs_in, cs), (hi_in, hi_tab), (lo_in, lo_tab),
        (w_in, w), (quen_in, quen),
    )
    for copy in copies[:8]:
        copy.wait()
    pick_x = picker(bx)
    pick_y = picker(by)
    rows_ref[...] = dot(cs[...], pick_x).astype(BF)
    xhi_ref[...] = dot(hi_tab[...], pick_x).astype(BF)
    xlo_ref[...] = dot(lo_tab[...], pick_x).astype(BF)
    yhi_ref[...] = dot(hi_tab[...], pick_y).astype(BF)
    ylo_ref[...] = dot(lo_tab[...], pick_y).astype(BF)
    table = dot_tn(pick_y, even[...])
    flip = jnp.where(iota((128, 1), 0) < BAND, 1.0, -1.0).astype(F32)
    cols_ref[:, 0:HALF] = (table * flip).astype(BF)
    cols_ref[:, HALF:TILE] = jnp.concatenate([table[BAND:], table[:BAND]], 0).astype(BF)
    sign = jnp.where(iota((1, 128), 1) < BAND, 1.0, -1.0).astype(F32)
    ends = dot(edge[...], pick_y)[0:8]
    ends = jnp.where(iota((8, 128), 0) < 4, sign * ends, pltpu.roll(pltpu.roll(ends, BAND, 1), 4, 0))
    count = placed_ref.shape[1] // 128
    own = iota((128, 128), 0) >> 3
    many = jnp.tile(ends, (16, 1))
    for k in range(count):
        placed_ref[:, 128 * k : 128 * (k + 1)] = jnp.where(own == k, many, 0.0).astype(BF)
        weight_ref[k : k + 1, :] = jnp.full((1, HALF), w[k], F32)
    copies[8].wait()
    pick = columns()
    for z in range(PLANES):
        side_ref[z] = dot_nt(pick, quen[z].astype(BF))


def spectrum_kernel(
    w_ref, got_ref, kern_ref, rows_ref, xhi_ref, xlo_ref, yhi_ref, ylo_ref, placed_ref, side_ref,
    big_ref, left_ref, right_ref, ring_ref,
):
    lane = iota((1, 128), 1)
    sign = jnp.where(lane < BAND, -1.0, 1.0).astype(F32)
    coarse = jnp.concatenate([got_ref[:, 0:32, :].reshape(256, 128), got_ref[:, 32:64, :].reshape(256, 128)], 1)
    summed = dot(coarse, yhi_ref[...]) + dot(coarse, ylo_ref[...])
    hi = summed.astype(BF)
    lo = (summed - hi.astype(F32)).astype(BF)
    u = (dot_tn(xhi_ref[...], hi) + dot_tn(xhi_ref[...], lo) + dot_tn(xlo_ref[...], hi)) * (1.0 / (TILE * TILE))
    v = u[:BAND] + sign * pltpu.roll(u[BAND:], BAND, 1)
    v_swap = pltpu.roll(v, BAND, 1)
    coef_a = jnp.where(lane < BAND, v, v_swap)
    coef_b = jnp.where(lane < BAND, v_swap, -v)
    count = kern_ref.shape[0]
    for k in range(count):
        cur = kern_ref[k].astype(F32)
        top = cur * coef_a + pltpu.roll(cur, BAND, 1) * coef_b
        big_ref[0:BAND, 128 * k : 128 * (k + 1)] = top.astype(BF)
        big_ref[BAND:128, 128 * k : 128 * (k + 1)] = (sign * pltpu.roll(top, BAND, 1)).astype(BF)
    narrow = dot_nt(placed_ref[...], big_ref[...]).astype(BF)
    field = dot_nt(narrow, rows_ref[...])
    total = jnp.zeros((8, TILE), F32)
    for k in range(count):
        part = field[8 * k : 8 * (k + 1)]
        total = total + w_ref[k : k + 1, 0:1] * (part * part)
    bright = total + pltpu.roll(total, 4, 0)
    place = iota((16, TILE), 0)
    eight = jnp.concatenate([bright, bright], 0)
    left_ref[0:16, :] = jnp.where(place < 2, eight, 0.0).astype(BF)
    right_ref[0:16, :] = jnp.where(place < 2, pltpu.roll(eight, 14, 0), 0.0).astype(BF)
    me = lax.axis_index("depth")
    before = lax.rem(me + 7, 8)
    after = lax.rem(me + 1, 8)
    for c in range(4):
        low = got_ref[after, 64 + 16 * c : 80 + 16 * c, :].astype(F32)
        high = got_ref[before, 64 + 16 * c : 80 + 16 * c, :].astype(F32)
        for z in range(PLANES):
            ring_ref[z, 2:6, 128 * c : 128 * (c + 1)] = jnp.zeros((4, 128), F32)
            for r in range(2):
                spot = 8 * r + z
                ring_ref[z, r : r + 1, 128 * c : 128 * (c + 1)] = low[spot : spot + 1]
                ring_ref[z, 6 + r : 7 + r, 128 * c : 128 * (c + 1)] = high[spot : spot + 1]
    left_ref[16:32, :] = jnp.zeros((16, TILE), BF)
    right_ref[16:32, :] = jnp.zeros((16, TILE), BF)
    ring = dot_nt(columns(), ring_ref[...].reshape(PLANES * 8, TILE).astype(BF))
    lefts, rights = [], []
    for z in range(PLANES):
        cols = jnp.concatenate([side_ref[z], ring if z == 0 else pltpu.roll(ring, STRIP - 8 * z, 1)], 1)
        lefts.append(cols[0:2])
        rights.append(cols[2:4])
    left_ref[16:32, 0:128] = jnp.concatenate(lefts, 0).astype(BF)
    right_ref[16:32, 0:128] = jnp.concatenate(rights, 0).astype(BF)


def image_kernel(w_ref, big_ref, rows_ref, cols_ref, img_ref):
    count = big_ref.shape[1] // 128
    chunk = 128
    cols = cols_ref[...]
    for part in range(TILE // chunk):
        half = dot(rows_ref[part * chunk : (part + 1) * chunk, :], big_ref[...]).astype(BF)
        total = jnp.zeros((chunk, HALF), F32)
        for k in range(count):
            field = dot(half[:, 128 * k : 128 * (k + 1)], cols)
            total = total + w_ref[k : k + 1, :] * (field[:, :HALF] * field[:, :HALF] + field[:, HALF:] * field[:, HALF:])
        img_ref[part * chunk : (part + 1) * chunk, :] = total


def pack_kernel(img_ref, from_left, from_right, out_ref, scr_ref):
    place = iota((8, TILE), 0)
    both = jnp.where(place < 2, from_left[0:16, :].astype(F32)[0:8], pltpu.roll(from_right[0:16, :].astype(F32)[0:8], 2, 0))
    lane = iota((8, HALF), 1)
    scr_ref[...] = jnp.zeros((16, HALF), F32)
    for p in range(8):
        base = p * STRIP
        out_ref[p, 0:STRIP, :] = img_ref[base : base + STRIP, :].astype(BF)
        nxt = (base + STRIP) % TILE
        scr_ref[0:2, :] = img_ref[nxt : nxt + 2, :]
        prv = (base - 2) % TILE
        scr_ref[6:8, :] = img_ref[prv : prv + 2, :]
        first = pltpu.roll(both, (TILE - base) % TILE, 1)[:, :HALF]
        second = pltpu.roll(both, (TILE - base + CYC) % TILE, 1)[:, :HALF]
        side = jnp.where(lane < 66, first, jnp.where(lane < CYC, second, 0.0))
        scr_ref[2:6, :] = side[0:4]
        out_ref[p, STRIP:80, :] = scr_ref[...].astype(BF)


def planes_side(source, spots):
    count = source.shape[0]
    row = iota((count, 128 * PLANES), 0)
    col = iota((count, 128 * PLANES), 1)
    z, lane = col >> 7, col & 127
    hit = row < 0
    for spot, place in zip(spots, (126, 127, 0, 1)):
        hit = hit | ((row == spot(z)) & (lane == place))
    return dot_tn(source, hit.astype(BF))


def acid_side(got_ref):
    tails = got_ref[:, 64:80, 0:128].reshape(16 * PLANES, 128)
    return planes_side(tails, [lambda z, j=j: 16 * z + 2 + j for j in range(4)])


def quen_side(from_left, from_right):
    both = jnp.concatenate([from_left[16:32, 0:128], from_right[16:32, 0:128]], 0)
    return planes_side(both, [lambda z, j=j: 2 * z + j for j in (0, 1, 16, 17)])


def exposed(intensity):
    return 1.0 - jnp.exp(-DILL_RATE * intensity)


def edge_kernel(got_ref, spread_ref, quen_in, from_left, from_right, tile_ref, m_ref, near, far, scr, sem):
    copies = fetch(sem, (quen_in.at[:, pl.ds(0, 8), :], near), (quen_in.at[:, pl.ds(STRIP - 8, 8), :], far))
    last = lax.axis_index("depth") == 7
    start = pl.multiple_of(jnp.where(last, STRIP - 16, 0), 16)
    coarse = jnp.concatenate([got_ref[z, pl.ds(start, 16), :] for z in range(PLANES)], 0)
    fine = exposed(dot(jnp.concatenate([coarse, coarse], 1), spread_ref[...]))
    side = acid_side(got_ref)
    side = exposed(jnp.where(last, side[STRIP - 8 : STRIP], side[0:8]))
    side_q = quen_side(from_left, from_right)
    side_q = jnp.where(last, side_q[STRIP - 8 : STRIP], side_q[0:8])
    for copy in copies:
        copy.wait()
    for z in range(PLANES):
        mine = fine[16 * z : 16 * (z + 1)]
        tile_ref[0, z, :, 0:TILE] = jnp.where(last, mine[8:16], mine[0:8])
        tile_ref[0, z, :, TILE:WIDE] = side[:, 128 * z : 128 * (z + 1)]
        tile_ref[1, z, :, 0:TILE] = jnp.where(last, far[z], near[z])
        tile_ref[1, z, :, TILE:WIDE] = side_q[:, 128 * z : 128 * (z + 1)]
    for f in range(2):
        for z in range(PLANES):
            outer = jnp.where(last, tile_ref[f, z, 6:8, :], tile_ref[f, z, 0:2, :])
            scr[16 * f + 2 * z : 16 * f + 2 * z + 2, :] = outer
    m_ref[...] = scr[...].astype(BF)


def moved(src_a, src_q, z, rows, cols):
    height, width = src_a.shape[1:]
    a = src_a[z, 0:rows, 0:cols]
    q = src_q[z, 0:rows, 0:cols]
    react = REACT_RATE * a * q

    def move(c, ref, lat, vert):
        up = ref[min(z + 1, PLANES - 1), 0:rows, 0:cols]
        down = ref[max(z - 1, 0), 0:rows, 0:cols]
        tall = ref[z, :, 0:cols]
        wide = ref[z, 0:rows, :]
        near = (pltpu.roll(tall, 1, 0) + pltpu.roll(tall, height - 1, 0))[0:rows]
        near = near + (pltpu.roll(wide, 1, 1)[:, 0:cols] + pltpu.roll(wide, width - 1, 1)[:, 0:cols])
        return (1.0 - 4.0 * lat - 2.0 * vert) * c + lat * near + vert * (up + down) - react

    return move(a, src_a, ACID_LAT, ACID_VERT), move(q, src_q, QUEN_LAT, QUEN_VERT)


def bake_kernel(
    got_ref, spread_ref, quen_in, ring_ref, from_left, from_right, a_out, q_out,
    a_ref, q_ref, a_mid, q_mid, a_end, q_end, sem,
):
    copy = pltpu.make_async_copy(quen_in, q_ref.at[:, pl.ds(0, STRIP), pl.ds(0, TILE)], sem.at[0, 0])
    copy.start()
    side = exposed(acid_side(got_ref))
    side_q = quen_side(from_left, from_right)
    coarse = got_ref[...].reshape(PLANES * 80, HALF)
    fine = dot(jnp.concatenate([coarse, coarse], 1), spread_ref[...])
    for z in range(PLANES):
        a_ref[z, :, 0:TILE] = exposed(fine[80 * z : 80 * z + CYC])
        a_ref[z, :, TILE:WIDE] = side[0:CYC, 128 * z : 128 * (z + 1)]
        q_ref[z, STRIP:CYC, 0:TILE] = ring_ref[z]
        q_ref[z, :, TILE:WIDE] = side_q[0:CYC, 128 * z : 128 * (z + 1)]
    copy.wait()
    for z in range(PLANES):
        a_mid[z], q_mid[z] = moved(a_ref, q_ref, z, CYC, WIDE)
    copies = []
    for z in range(PLANES):
        a_end[z], q_end[z] = moved(a_mid, q_mid, z, STRIP, TILE)
        for i, (src, dst) in enumerate(((a_end, a_out), (q_end, q_out))):
            copies.append(pltpu.make_async_copy(src.at[z], dst.at[z], sem.at[1 + i, z]))
            copies[-1].start()
    for copy in copies:
        copy.wait()


def patch_kernel(tile_ref, m_ref, a_in, q_in, a_out, q_out, a_ref, q_ref, a_mid, q_mid, a_end, q_end, sem):
    level = lax.axis_index("depth")
    last = level == 7

    def redo(start, outer, away):
        spot = pl.ds(start, 8)
        copies = [
            pltpu.make_async_copy(a_out.at[:, spot, :], a_end, sem.at[0]),
            pltpu.make_async_copy(q_out.at[:, spot, :], q_end, sem.at[1]),
        ]
        for copy in copies:
            copy.start()
        m = m_ref[...].astype(F32)
        for z in range(PLANES):
            for f, ref in ((0, a_ref), (1, q_ref)):
                ref[z, 0:8, :] = tile_ref[f, z]
                ref[z, 8:16, :] = jnp.zeros((8, WIDE), F32)
                ref[z, away : away + 2, :] = m[16 * f + 2 * z : 16 * f + 2 * z + 2]
        for z in range(PLANES):
            a_mid[z], q_mid[z] = moved(a_ref, q_ref, z, 16, WIDE)
        for copy in copies:
            copy.wait()
        for z in range(PLANES):
            a, q = moved(a_mid, q_mid, z, 8, TILE)
            a_end[z, outer : outer + 2, :] = a[outer : outer + 2]
            q_end[z, outer : outer + 2, :] = q[outer : outer + 2]
        copies = [
            pltpu.make_async_copy(a_end, a_out.at[:, spot, :], sem.at[2]),
            pltpu.make_async_copy(q_end, q_out.at[:, spot, :], sem.at[3]),
        ]
        for copy in copies:
            copy.start()
        for copy in copies:
            copy.wait()

    @pl.when(level == 0)
    def _():
        redo(0, 0, 14)

    @pl.when(last)
    def _():
        redo(STRIP - 8, 6, 8)


ANY = pl.BlockSpec(memory_space=pl.ANY)
HBM = pl.BlockSpec(memory_space=pltpu.HBM)


def call(kernel, out, specs, scratch=(), outs=None, flops=0, size=0, limit=LIMIT, **more):
    return pl.pallas_call(
        kernel,
        out_shape=out,
        in_specs=specs,
        out_specs=jax.tree.map(lambda _: VMEM, out) if outs is None else outs,
        scratch_shapes=scratch,
        compiler_params=pltpu.CompilerParams(vmem_limit_bytes=limit),
        cost_estimate=pl.CostEstimate(flops=flops, bytes_accessed=size, transcendentals=0),
        **more,
    )


def on_device(sizes, mask, kernels, weights, band_rows, band_cols, quencher):
    n_depth, n_tx, n_ty = sizes
    con = constants()
    count = kernels.shape[1]
    shape = jax.ShapeDtypeStruct
    dma = pltpu.SemaphoreType.DMA
    bx = band_rows.reshape(1, BAND)
    by = band_cols.reshape(1, BAND)
    quen = quencher[:, 0]
    table = pltpu.VMEM((256, 256), BF)
    band = pltpu.VMEM((1, BAND), jnp.int32)

    packed = call(
        strip_kernel, shape((8, 128, 128), BF), [HBM] * 2, limit=MOST,
        scratch=[
            pltpu.VMEM((4, STRIP, 128), jnp.int32), pltpu.VMEM((PLANES, 8, TILE), F32),
            pltpu.VMEM((PLANES, 8, TILE), F32), pltpu.VMEM((32, TILE), F32), dma((6,)),
        ],
    )(mask[0], quen)
    got = lax.all_to_all(packed, "depth", 0, 0, tiled=True)
    *tables, cols, placed, side, weight = call(
        table_kernel,
        (
            shape((TILE, 128), BF), *[shape((256, 128), BF)] * 4, shape((128, TILE), BF),
            shape((128, 128 * count), BF), shape((PLANES, 16, STRIP), F32), shape((16, HALF), F32),
        ),
        [ANY] + [HBM] * 9,
        scratch=[
            band, band, pltpu.VMEM((TILE, 256), BF), table, table, table, pltpu.VMEM((16, 256), BF),
            pltpu.VMEM((PLANES, STRIP, TILE), F32), pltpu.SMEM((count,), F32), dma((9,)),
        ],
        flops=400_000_000, size=2_000_000,
    )(packed, bx, by, con["cs"], con["pairs_hi"], con["pairs_lo"], con["even_t"], con["edge"], quen, weights)
    rows = tables[0]
    big, left, right, ring = call(
        spectrum_kernel,
        (
            shape((128, 128 * count), BF), shape((32, TILE), BF), shape((32, TILE), BF),
            shape((PLANES, 8, TILE), F32),
        ),
        [VMEM] * 10,
    )(weight, got, kernels[0], *tables, placed, side)
    from_right = lax.ppermute(left, "ty", [(i, (i - 1) % n_ty) for i in range(n_ty)])
    from_left = lax.ppermute(right, "ty", [(i, (i + 1) % n_ty) for i in range(n_ty)])
    image = call(
        image_kernel, shape((TILE, HALF), F32), [VMEM] * 4, flops=2_400_000_000, size=2_000_000,
    )(weight, big, rows, cols)
    strips = call(
        pack_kernel, shape((8, 80, HALF), BF), [VMEM] * 3, scratch=[pltpu.VMEM((16, HALF), F32)],
    )(image, from_left, from_right)
    planes = lax.all_to_all(strips, "depth", 0, 0, tiled=True)
    tile = pltpu.VMEM((PLANES, 8, TILE), F32)
    edge, outer = call(
        edge_kernel, (shape((2, PLANES, 8, WIDE), F32), shape((32, WIDE), BF)), [VMEM] * 2 + [HBM] + [VMEM] * 2,
        scratch=[tile, tile, pltpu.VMEM((32, WIDE), F32), dma((2,))],
    )(planes, con["spread"], quen, from_left, from_right)
    pairs = []
    for t in range(n_tx):
        low, high = (n_depth - 1) * n_tx + t, (t + 1) % n_tx
        pairs += [(low, high), (high, low)]
    outer = lax.ppermute(outer, ("depth", "tx"), pairs)
    out = shape((PLANES, STRIP, TILE), F32)
    wide = pltpu.VMEM((PLANES, CYC, WIDE), F32)
    end = pltpu.VMEM((PLANES, STRIP, TILE), F32)
    acid, left_over = call(
        bake_kernel, (out, out), [VMEM] * 2 + [HBM] + [VMEM] * 3, outs=(HBM, HBM),
        scratch=[wide, wide, wide, wide, end, end, dma((3, PLANES))], flops=3_000_000_000, size=4_000_000,
    )(planes, con["spread"], quen, ring, from_left, from_right)
    low = pltpu.VMEM((PLANES, 16, WIDE), F32)
    acid, left_over = call(
        patch_kernel, (out, out), [VMEM] * 2 + [HBM] * 2, outs=(HBM, HBM),
        scratch=[low, low, low, low, tile, tile, dma((4,))], input_output_aliases={2: 0, 3: 1},
    )(edge, outer, acid, left_over)
    return acid[:, None], left_over[:, None]


def solution(mesh):
    sizes = (mesh.shape["depth"], mesh.shape["tx"], mesh.shape["ty"])
    placed = (
        P("tx", "depth", "ty"),
        P("depth", None, None, None),
        P(),
        P(),
        P(),
        P(None, "tx", "depth", "ty"),
    )
    return jax.shard_map(
        functools.partial(on_device, sizes),
        mesh=mesh,
        in_specs=placed,
        out_specs=(P(None, "tx", "depth", "ty"), P(None, "tx", "depth", "ty")),
        check_vma=False,
    )
```

```python
import functools
import math

import jax
import jax.numpy as jnp
import numpy as np
from jax import lax
from jax.experimental import pallas as pl
from jax.experimental.pallas import tpu as pltpu
from jax.sharding import PartitionSpec as P

BF = jnp.bfloat16
F32 = jnp.float32
TILE = 512
BAND = 64
HALF = 256
PLANES = 8
STRIP = 64
CYC = 72
WIDE = 640
DILL_RATE = 1.0
REACT_RATE = 0.4
ACID_LAT, ACID_VERT = 0.23, 0.03
QUEN_LAT, QUEN_VERT = 0.15, 0.05
VMEM = pl.BlockSpec(memory_space=pltpu.VMEM)
SMEM = pl.BlockSpec(memory_space=pltpu.SMEM)
LIMIT = 40 * 1024 * 1024
MOST = 60 * 1024 * 1024


def split(x):
    hi = np.asarray(x, np.float32).astype(jnp.bfloat16)
    lo = (np.asarray(x, np.float64) - hi.astype(np.float64)).astype(np.float32).astype(jnp.bfloat16)
    return hi, lo


@functools.cache
def constants():
    u = np.arange(TILE)
    f = np.arange(128) - BAND // 2
    angle = np.mod(u[:, None] * f[None, :], TILE) * (2.0 * np.pi / TILE)
    cs = np.concatenate([np.cos(angle), np.sin(angle)], 1)
    n = np.arange(HALF)
    m = np.arange(1, 128)
    gap = np.mod(u[None, :] - 2 * n[:, None], TILE)
    line = (1.0 + 2.0 * np.cos(2.0 * np.pi * m[None, :] * u[:, None] / TILE).sum(1)) / HALF
    spread = line[gap]
    spread[:, 0::2] = np.eye(HALF)
    out = {}
    out["cs"] = split(cs)[0]
    out["pairs_hi"], out["pairs_lo"] = split(cs[0::2] + cs[1::2])
    out["even_t"] = split(cs[0::2].T)[0]
    edge = np.zeros((16, 256))
    edge[:4] = cs[[0, 1, TILE - 2, TILE - 1]]
    out["edge"] = split(edge)[0]
    out["spread"] = np.concatenate(split(spread), 0)
    return out


def dot(a, b):
    return lax.dot_general(a, b, (((1,), (0,)), ((), ())), preferred_element_type=F32)


def dot_nt(a, b):
    return lax.dot_general(a, b, (((1,), (1,)), ((), ())), preferred_element_type=F32)


def dot_tn(a, b):
    return lax.dot_general(a, b, (((0,), (0,)), ((), ())), preferred_element_type=F32)


def iota(shape, dim):
    return lax.broadcasted_iota(jnp.int32, shape, dim)


def fetch(sem, *pairs):
    copies = [pltpu.make_async_copy(src, dst, sem.at[i]) for i, (src, dst) in enumerate(pairs)]
    for copy in copies:
        copy.start()
    return copies


def picker(band_ref):
    band = band_ref[...]
    return (iota((256, 128), 0) == jnp.concatenate([band, band + 128], 1)).astype(BF)


def columns():
    row = iota((16, TILE), 0)
    col = jnp.where(row < 2, row, row + TILE - 4)
    return ((iota((16, TILE), 1) == col) & (row < 4)).astype(BF)


def strip_kernel(mask_in, quen_in, out_ref, mask, head, tail, edge, sem):
    copies = fetch(
        sem, *[(mask_in.at[:, pl.ds(128 * c, 128)], mask.at[c]) for c in range(4)],
        (quen_in.at[:, pl.ds(0, 8), :], head), (quen_in.at[:, pl.ds(STRIP - 8, 8), :], tail),
    )
    halves = (iota((TILE, HALF), 0) == 2 * iota((TILE, HALF), 1)).astype(BF)
    for copy in copies[:4]:
        copy.wait()
    rows = [mask[c, pl.ds(0, STRIP // 2, stride=2), :] for c in range(4)]
    coarse = dot(jnp.concatenate(rows, 1).astype(F32).astype(BF), halves).astype(BF)
    for copy in copies[4:]:
        copy.wait()
    for peer in range(8):
        out_ref[peer, 0:32, :] = coarse[:, 0:128]
        out_ref[peer, 32:64, :] = coarse[:, 128:256]
        for k, c in enumerate((0, 2, 1, 3)):
            edge[peer, 4 * k : 4 * k + 2, :] = head[peer, 0:2, 128 * c : 128 * (c + 1)]
            edge[peer, 4 * k + 2 : 4 * k + 4, :] = tail[peer, 6:8, 128 * c : 128 * (c + 1)]
        out_ref[peer, 64:80, :] = edge[peer].astype(BF)


def table_kernel(
    after, bx_in, by_in, cs_in, hi_in, lo_in, even_in, edge_in, quen_in, w_in,
    rows_ref, xhi_ref, xlo_ref, yhi_ref, ylo_ref, cols_ref, placed_ref, left_ref, right_ref, weight_ref,
    bx, by, cs, hi_tab, lo_tab, even, edge, quen, w, sem,
):
    copies = fetch(
        sem, (bx_in, bx), (by_in, by), (edge_in, edge), (even_in, even), (cs_in, cs), (hi_in, hi_tab), (lo_in, lo_tab),
        (w_in, w), (quen_in, quen),
    )
    for copy in copies[:8]:
        copy.wait()
    pick_x = picker(bx)
    pick_y = picker(by)
    rows_ref[...] = dot(cs[...], pick_x).astype(BF)
    xhi_ref[...] = dot(hi_tab[...], pick_x).astype(BF)
    xlo_ref[...] = dot(lo_tab[...], pick_x).astype(BF)
    yhi_ref[...] = dot(hi_tab[...], pick_y).astype(BF)
    ylo_ref[...] = dot(lo_tab[...], pick_y).astype(BF)
    table = dot_tn(pick_y, even[...])
    flip = jnp.where(iota((128, 1), 0) < BAND, 1.0, -1.0).astype(F32)
    cols_ref[:, 0:HALF] = (table * flip).astype(BF)
    cols_ref[:, HALF:TILE] = jnp.concatenate([table[BAND:], table[:BAND]], 0).astype(BF)
    sign = jnp.where(iota((1, 128), 1) < BAND, 1.0, -1.0).astype(F32)
    ends = dot(edge[...], pick_y)[0:8]
    ends = jnp.where(iota((8, 128), 0) < 4, sign * ends, pltpu.roll(pltpu.roll(ends, BAND, 1), 4, 0))
    count = placed_ref.shape[1] // 128
    own = iota((128, 128), 0) >> 3
    many = jnp.tile(ends, (16, 1))
    for k in range(count):
        placed_ref[:, 128 * k : 128 * (k + 1)] = jnp.where(own == k, many, 0.0).astype(BF)
        weight_ref[k : k + 1, :] = jnp.full((1, HALF), w[k], F32)
    copies[8].wait()
    ends = dot_nt(columns(), quen[...].reshape(PLANES * STRIP, TILE).astype(BF))
    for low, ref in ((0, left_ref), (2, right_ref)):
        ref[...] = jnp.zeros((16, 128), F32)
        for z in range(PLANES):
            ref[2 * z : 2 * z + 2, 0:STRIP] = ends[low : low + 2, STRIP * z : STRIP * (z + 1)]


def spectrum_kernel(
    w_ref, got_ref, kern_ref, rows_ref, xhi_ref, xlo_ref, yhi_ref, ylo_ref, placed_ref, qleft_ref, qright_ref,
    big_ref, left_ref, right_ref, ring_ref,
):
    lane = iota((1, 128), 1)
    sign = jnp.where(lane < BAND, -1.0, 1.0).astype(F32)
    coarse = jnp.concatenate([got_ref[:, 0:32, :].reshape(256, 128), got_ref[:, 32:64, :].reshape(256, 128)], 1)
    summed = dot(coarse, yhi_ref[...]) + dot(coarse, ylo_ref[...])
    hi = summed.astype(BF)
    lo = (summed - hi.astype(F32)).astype(BF)
    u = (dot_tn(xhi_ref[...], hi) + dot_tn(xhi_ref[...], lo) + dot_tn(xlo_ref[...], hi)) * (1.0 / (TILE * TILE))
    v = u[:BAND] + sign * pltpu.roll(u[BAND:], BAND, 1)
    v_swap = pltpu.roll(v, BAND, 1)
    coef_a = jnp.where(lane < BAND, v, v_swap)
    coef_b = jnp.where(lane < BAND, v_swap, -v)
    count = kern_ref.shape[0]
    for k in range(count):
        cur = kern_ref[k].astype(F32)
        top = cur * coef_a + pltpu.roll(cur, BAND, 1) * coef_b
        big_ref[0:BAND, 128 * k : 128 * (k + 1)] = top.astype(BF)
        big_ref[BAND:128, 128 * k : 128 * (k + 1)] = (sign * pltpu.roll(top, BAND, 1)).astype(BF)
    narrow = dot_nt(placed_ref[...], big_ref[...]).astype(BF)
    field = dot_nt(narrow, rows_ref[...])
    total = jnp.zeros((8, TILE), F32)
    for k in range(count):
        part = field[8 * k : 8 * (k + 1)]
        total = total + w_ref[k : k + 1, 0:1] * (part * part)
    bright = total + pltpu.roll(total, 4, 0)
    place = iota((16, TILE), 0)
    eight = jnp.concatenate([bright, bright], 0)
    left_ref[0:16, :] = jnp.where(place < 2, eight, 0.0).astype(BF)
    right_ref[0:16, :] = jnp.where(place < 2, pltpu.roll(eight, 14, 0), 0.0).astype(BF)
    for ref, cols in ((left_ref, qleft_ref), (right_ref, qright_ref)):
        ref[16:32, 0:128] = cols[...].astype(BF)
        ref[16:32, 128:TILE] = jnp.zeros((16, TILE - 128), BF)
    beyond = (iota((16, 128), 0) & 3) < 2
    heard = [got_ref[p, 64:80, :].astype(F32) for p in range(8)]
    for p in range(0, 8, 2):
        pair = [jnp.where(beyond, heard[(d + 1) % 8], heard[(d + 7) % 8]) for d in (p, p + 1)]
        for d, ring in zip((p, p + 1), pair):
            ring_ref[d, :, 0:128] = ring[0:8]
            ring_ref[d, :, 128:256] = ring[8:16]
        left_ref[32:48, 64 * p : 64 * p + 128] = jnp.concatenate([pair[0][0:8], pair[1][0:8]], 0).astype(BF)
        right_ref[32:48, 64 * p : 64 * p + 128] = jnp.concatenate([pair[0][8:16], pair[1][8:16]], 0).astype(BF)


def image_kernel(w_ref, big_ref, rows_ref, cols_ref, img_ref):
    count = big_ref.shape[1] // 128
    chunk = 128
    cols = cols_ref[...]
    for part in range(TILE // chunk):
        half = dot(rows_ref[part * chunk : (part + 1) * chunk, :], big_ref[...]).astype(BF)
        total = jnp.zeros((chunk, HALF), F32)
        for k in range(count):
            field = dot(half[:, 128 * k : 128 * (k + 1)], cols)
            total = total + w_ref[k : k + 1, :] * (field[:, :HALF] * field[:, :HALF] + field[:, HALF:] * field[:, HALF:])
        img_ref[part * chunk : (part + 1) * chunk, :] = total


def pack_kernel(img_ref, ring_ref, from_left, from_right, out_ref, scr_ref):
    place = iota((8, TILE), 0)
    both = jnp.where(place < 2, from_left[0:16, :].astype(F32)[0:8], pltpu.roll(from_right[0:16, :].astype(F32)[0:8], 2, 0))
    far = from_left[32:48, :].astype(F32)
    near = from_right[32:48, :].astype(F32)
    lane = iota((8, 128), 1)
    for p in range(8):
        base = p * STRIP
        out_ref[p, 0:STRIP, :] = img_ref[base : base + STRIP, :].astype(BF)
        nxt = (base + STRIP) % TILE
        scr_ref[0:2, :] = img_ref[nxt : nxt + 2, :]
        prv = (base - 2) % TILE
        scr_ref[6:8, :] = img_ref[prv : prv + 2, :]
        first = pltpu.roll(both, (TILE - base) % TILE, 1)[:, 0:128]
        second = pltpu.roll(both, (TILE - base + CYC) % TILE, 1)[:, 0:128]
        side = jnp.where(lane < 66, first, jnp.where(lane < CYC, second, 0.0))
        scr_ref[2:6, 0:128] = side[0:4]
        spot, cols = 8 * (p & 1), slice(128 * (p >> 1), 128 * (p >> 1) + 128)
        corner = jnp.where(lane < STRIP, near[spot : spot + 8, cols], pltpu.roll(far[spot : spot + 8, cols], 4, 0))
        scr_ref[2:6, 128:HALF] = corner[0:4]
        scr_ref[8:16, :] = ring_ref[p]
        out_ref[p, STRIP:80, :] = scr_ref[...].astype(BF)


def acid_side(got_ref):
    return got_ref[:, 64:80, 0:128].astype(F32).reshape(16 * PLANES, 128).T


def acid_cols(side, z):
    return pltpu.roll(side, (124 - 16 * z) % 128, 1)


def quen_side(from_left, from_right):
    both = [from_left[16:32, 0:128].astype(F32), from_right[16:32, 0:128].astype(F32), jnp.zeros((96, 128), F32)]
    return jnp.concatenate(both, 0).T


def quen_cols(side, z):
    behind = iota((1, 128), 1) >= STRIP
    return jnp.where(behind, pltpu.roll(side, (126 - 2 * z) % 128, 1), pltpu.roll(side, (112 - 2 * z) % 128, 1))


def exposed(intensity):
    return 1.0 - jnp.exp(-DILL_RATE * intensity)


def edge_kernel(after, got_ref, spread_ref, quen_in, from_left, from_right, tile_ref, m_ref, near, far, scr, sem):
    copies = fetch(sem, (quen_in.at[:, pl.ds(0, 8), :], near), (quen_in.at[:, pl.ds(STRIP - 8, 8), :], far))
    last = lax.axis_index("depth") == 7
    start = pl.multiple_of(jnp.where(last, STRIP - 16, 0), 16)
    coarse = [got_ref[z, pl.ds(start, 16), :] for z in range(PLANES)] + [got_ref[z, 64:80, :] for z in range(PLANES)]
    coarse = jnp.concatenate(coarse, 0)
    fine = exposed(dot(jnp.concatenate([coarse, coarse], 1), spread_ref[...]))
    side = acid_side(got_ref)
    side = exposed(jnp.concatenate([jnp.where(last, side[STRIP - 8 : STRIP], side[0:8]), side[STRIP:CYC]], 0))
    side_q = quen_side(from_left, from_right)
    side_q = jnp.where(last, side_q[STRIP - 8 : STRIP], side_q[0:8])
    for z in range(PLANES):
        outer = acid_cols(side, z)
        mine = fine[16 * z : 16 * (z + 1)]
        tile_ref[0, z, :, 0:TILE] = jnp.where(last, mine[8:16], mine[0:8])
        tile_ref[0, z, :, TILE:WIDE] = outer[0:8]
        tile_ref[1, z, :, TILE:WIDE] = quen_cols(side_q, z)
        ring = got_ref[z, 64:80, :].astype(F32)
        back = fine[128 + 16 * z : 136 + 16 * z]
        place = slice(2 * z, 2 * z + 2)
        scr[place, 0:TILE] = jnp.where(last, back[0:2], back[6:8])
        scr[place, TILE:WIDE] = jnp.where(last, outer[8:10], outer[14:16])
        place = slice(16 + 2 * z, 18 + 2 * z)
        scr[place, 0:HALF] = jnp.where(last, ring[8:10], ring[10:12])
        scr[place, HALF:TILE] = jnp.where(last, ring[12:14], ring[14:16])
        scr[place, TILE:WIDE] = jnp.where(last, ring[2:4, 128:HALF], ring[4:6, 128:HALF])
    m_ref[...] = scr[...].astype(BF)
    for copy in copies:
        copy.wait()
    for z in range(PLANES):
        tile_ref[1, z, :, 0:TILE] = jnp.where(last, far[z], near[z])


def moved(src_a, src_q, z, t, cols):
    tiles, width = src_a.shape[1] // 8, src_a.shape[2]
    here, before, after = (pl.ds(8 * (i % tiles), 8) for i in (t, t - 1, t + 1))
    row = iota((8, 1), 0)
    a = src_a[z, here, 0:cols]
    q = src_q[z, here, 0:cols]
    react = REACT_RATE * a * q

    def move(c, ref, lat, vert):
        up = ref[min(z + 1, PLANES - 1), here, 0:cols]
        down = ref[max(z - 1, 0), here, 0:cols]
        wide = ref[z, here, :]
        near = pltpu.roll(jnp.where(row == 7, ref[z, before, 0:cols], c), 1, 0)
        near = near + pltpu.roll(jnp.where(row == 0, ref[z, after, 0:cols], c), 7, 0)
        near = near + (pltpu.roll(wide, 1, 1)[:, 0:cols] + pltpu.roll(wide, width - 1, 1)[:, 0:cols])
        return (1.0 - 4.0 * lat - 2.0 * vert) * c + lat * near + vert * (up + down) - react

    return move(a, src_a, ACID_LAT, ACID_VERT), move(q, src_q, QUEN_LAT, QUEN_VERT)


def bake_kernel(
    turn, got_ref, spread_ref, quen_ref, from_left, from_right, *refs,
):
    a_out, q_out, rim_ref, a_ref, q_ref, a_mid, q_mid, a_end, q_end, sem = refs[-10:]

    @pl.when((lax.axis_index("tx") & 1) == turn)
    def _():
        side = exposed(acid_side(got_ref)[0:CYC])
        side_q = quen_side(from_left, from_right)[0:STRIP]
        coarse = got_ref[...].reshape(PLANES * 80, HALF)
        fine = dot(jnp.concatenate([coarse, coarse], 1), spread_ref[...])
        for z in range(PLANES):
            a_ref[z, :, 0:TILE] = exposed(fine[80 * z : 80 * z + CYC])
            a_ref[z, :, TILE:WIDE] = acid_cols(side, z)
            q_ref[z, 0:STRIP, 0:TILE] = quen_ref[z]
            q_ref[z, 0:STRIP, TILE:WIDE] = quen_cols(side_q, z)
            ring = got_ref[z, STRIP:80, :].astype(F32)
            q_ref[z, STRIP:CYC, :] = jnp.zeros((8, WIDE), F32)
            for i, row in ((0, STRIP), (2, 70)):
                q_ref[z, row : row + 2, 0:HALF] = ring[8 + i : 10 + i]
                q_ref[z, row : row + 2, HALF:TILE] = ring[12 + i : 14 + i]
                q_ref[z, row : row + 2, TILE:WIDE] = ring[2 + i : 4 + i, 128:HALF]
        for z in range(PLANES):
            for t in range(CYC // 8):
                spot = pl.ds(8 * t, 8)
                a_mid[z, spot, :], q_mid[z, spot, :] = moved(a_ref, q_ref, z, t, WIDE)
        copies = []
        for z in range(PLANES):
            for t in range(STRIP // 8):
                spot = pl.ds(8 * t, 8)
                a_end[z, spot, :], q_end[z, spot, :] = moved(a_mid, q_mid, z, t, TILE)
            for i, (src, dst) in enumerate(((a_end, a_out), (q_end, q_out))):
                copies.append(pltpu.make_async_copy(src.at[z], dst.at[z], sem.at[i, z]))
                copies[-1].start()
        level = lax.axis_index("depth")
        for edge, start in ((0, 0), (7, STRIP - 8)):

            @pl.when(level == edge)
            def _():
                rim_ref[0] = a_end[:, start : start + 8, :]
                rim_ref[1] = q_end[:, start : start + 8, :]

        for copy in copies:
            copy.wait()


def patch_kernel(tile_ref, m_ref, rim_even, rim_odd, a_in, q_in, a_out, q_out, a_ref, q_ref, a_mid, q_mid, a_end, q_end, sem):
    level = lax.axis_index("depth")
    last = level == 7

    @pl.when((level == 0) | last)
    def _():
        spot = pl.ds(pl.multiple_of(jnp.where(last, STRIP - 8, 0), 8), 8)
        row = iota((8, 1), 0)
        heard = jnp.where(last, row - 2, 5 - row) < 0
        mine = jnp.where(last, row - 6, 1 - row) >= 0
        m = m_ref[...].astype(F32)
        for z in range(PLANES):
            for f, ref in ((0, a_ref), (1, q_ref)):
                pair = m[16 * f + 2 * z : 16 * f + 2 * z + 2]
                ref[z] = jnp.where(heard, jnp.concatenate([pair] * 4, 0), tile_ref[f, z])
        for z in range(PLANES):
            a_mid[z], q_mid[z] = moved(a_ref, q_ref, z, 0, WIDE)
        odd = (lax.axis_index("tx") & 1) == 1
        for z in range(PLANES):
            a, q = moved(a_mid, q_mid, z, 0, TILE)
            a_end[z] = jnp.where(mine, a, jnp.where(odd, rim_odd[0, z], rim_even[0, z]))
            q_end[z] = jnp.where(mine, q, jnp.where(odd, rim_odd[1, z], rim_even[1, z]))
        for copy in fetch(sem, (a_end, a_out.at[:, spot, :]), (q_end, q_out.at[:, spot, :])):
            copy.wait()


ANY = pl.BlockSpec(memory_space=pl.ANY)
HBM = pl.BlockSpec(memory_space=pltpu.HBM)


def call(kernel, out, specs, scratch=(), outs=None, flops=0, size=0, limit=LIMIT, **more):
    return pl.pallas_call(
        kernel,
        out_shape=out,
        in_specs=specs,
        out_specs=jax.tree.map(lambda _: VMEM, out) if outs is None else outs,
        scratch_shapes=scratch,
        compiler_params=pltpu.CompilerParams(vmem_limit_bytes=limit),
        cost_estimate=pl.CostEstimate(flops=flops, bytes_accessed=size, transcendentals=0),
        **more,
    )


def on_device(sizes, mask, kernels, weights, band_rows, band_cols, quencher):
    n_depth, n_tx, n_ty = sizes
    con = constants()
    count = kernels.shape[1]
    shape = jax.ShapeDtypeStruct
    dma = pltpu.SemaphoreType.DMA
    bx = band_rows.reshape(1, BAND)
    by = band_cols.reshape(1, BAND)
    quen = quencher[:, 0]
    table = pltpu.VMEM((256, 256), BF)
    band = pltpu.VMEM((1, BAND), jnp.int32)

    packed = call(
        strip_kernel, shape((8, 80, 128), BF), [HBM] * 2, limit=MOST,
        scratch=[
            pltpu.VMEM((4, STRIP, 128), jnp.int32), pltpu.VMEM((PLANES, 8, TILE), F32),
            pltpu.VMEM((PLANES, 8, TILE), F32), pltpu.VMEM((8, 16, 128), F32), dma((6,)),
        ],
    )(mask[0], quen)
    got = lax.all_to_all(packed, "depth", 0, 0, tiled=True)
    *tables, cols, placed, qleft, qright, weight = call(
        table_kernel,
        (
            shape((TILE, 128), BF), *[shape((256, 128), BF)] * 4, shape((128, TILE), BF),
            shape((128, 128 * count), BF), shape((16, 128), F32), shape((16, 128), F32), shape((16, HALF), F32),
        ),
        [ANY] + [HBM] * 9,
        scratch=[
            band, band, pltpu.VMEM((TILE, 256), BF), table, table, table, pltpu.VMEM((16, 256), BF),
            pltpu.VMEM((PLANES, STRIP, TILE), F32), pltpu.SMEM((count,), F32), dma((9,)),
        ],
        flops=400_000_000, size=2_000_000,
    )(packed, bx, by, con["cs"], con["pairs_hi"], con["pairs_lo"], con["even_t"], con["edge"], quen, weights)
    rows = tables[0]
    big, left, right, ring = call(
        spectrum_kernel,
        (
            shape((128, 128 * count), BF), shape((48, TILE), BF), shape((48, TILE), BF),
            shape((8, 8, HALF), F32),
        ),
        [VMEM] * 11,
    )(weight, got, kernels[0], *tables, placed, qleft, qright)
    from_right = lax.ppermute(left, "ty", [(i, (i - 1) % n_ty) for i in range(n_ty)])
    from_left = lax.ppermute(right, "ty", [(i, (i + 1) % n_ty) for i in range(n_ty)])
    image = call(
        image_kernel, shape((TILE, HALF), F32), [VMEM] * 4, flops=2_400_000_000, size=2_000_000,
    )(weight, big, rows, cols)
    strips = call(
        pack_kernel, shape((8, 80, HALF), BF), [VMEM] * 4, scratch=[pltpu.VMEM((16, HALF), F32)],
    )(image, ring, from_left, from_right)
    planes = lax.all_to_all(strips, "depth", 0, 0, tiled=True)
    tile = pltpu.VMEM((PLANES, 8, TILE), F32)
    out = shape((PLANES, STRIP, TILE), F32)
    wide = pltpu.VMEM((PLANES, CYC, WIDE), F32)
    done = pltpu.VMEM((PLANES, STRIP, TILE), F32)

    def bake(turn, *before):
        return call(
            functools.partial(bake_kernel, turn), (out, out, shape((2, PLANES, 8, TILE), F32)),
            [VMEM] * 5 + [HBM] * len(before), outs=(HBM, HBM, VMEM),
            scratch=[wide, wide, wide, wide, done, done, dma((2, PLANES))], flops=3_000_000_000, size=4_000_000,
            input_output_aliases={5 + i: i for i in range(len(before))},
        )(planes, con["spread"], quen, from_left, from_right, *before)

    acid, left_over, rim_odd = bake(1)
    edge, outer = call(
        edge_kernel, (shape((2, PLANES, 8, WIDE), F32), shape((32, WIDE), BF)), [ANY] + [VMEM] * 2 + [HBM] + [VMEM] * 2,
        scratch=[tile, tile, pltpu.VMEM((32, WIDE), F32), dma((2,))],
    )(rim_odd, planes, con["spread"], quen, from_left, from_right)
    end = (n_depth - 1) * n_tx
    pairs = [(t, (t + 1) % n_tx) for t in range(n_tx)] + [(end + t, end + (t - 1) % n_tx) for t in range(n_tx)]
    outer = lax.ppermute(outer, ("depth", "tx"), pairs)
    acid, left_over, rim_even = bake(0, acid, left_over)
    low = pltpu.VMEM((PLANES, 8, WIDE), F32)
    acid, left_over = call(
        patch_kernel, (out, out), [VMEM] * 4 + [HBM] * 2, outs=(HBM, HBM),
        scratch=[low, low, low, low, tile, tile, dma((2,))], input_output_aliases={4: 0, 5: 1},
    )(edge, outer, rim_even, rim_odd, acid, left_over)
    return acid[:, None], left_over[:, None]


def solution(mesh):
    sizes = (mesh.shape["depth"], mesh.shape["tx"], mesh.shape["ty"])
    placed = (
        P("tx", "depth", "ty"),
        P("depth", None, None, None),
        P(),
        P(),
        P(),
        P(None, "tx", "depth", "ty"),
    )
    return jax.shard_map(
        functools.partial(on_device, sizes),
        mesh=mesh,
        in_specs=placed,
        out_specs=(P(None, "tx", "depth", "ty"), P(None, "tx", "depth", "ty")),
        check_vma=False,
    )
```

```python
import functools
import math

import jax
import jax.numpy as jnp
import numpy as np
from jax import lax
from jax.experimental import pallas as pl
from jax.experimental.pallas import tpu as pltpu
from jax.sharding import PartitionSpec as P

BF = jnp.bfloat16
F32 = jnp.float32
TILE = 512
BAND = 64
HALF = 256
PLANES = 8
STRIP = 64
CYC = 72
WIDE = 640
DILL_RATE = 1.0
REACT_RATE = 0.4
ACID_LAT, ACID_VERT = 0.23, 0.03
QUEN_LAT, QUEN_VERT = 0.15, 0.05
VMEM = pl.BlockSpec(memory_space=pltpu.VMEM)
SMEM = pl.BlockSpec(memory_space=pltpu.SMEM)
LIMIT = 40 * 1024 * 1024
MOST = 60 * 1024 * 1024


def split(x):
    hi = np.asarray(x, np.float32).astype(jnp.bfloat16)
    lo = (np.asarray(x, np.float64) - hi.astype(np.float64)).astype(np.float32).astype(jnp.bfloat16)
    return hi, lo


@functools.cache
def constants():
    u = np.arange(TILE)
    f = np.arange(128) - BAND // 2
    angle = np.mod(u[:, None] * f[None, :], TILE) * (2.0 * np.pi / TILE)
    cs = np.concatenate([np.cos(angle), np.sin(angle)], 1)
    n = np.arange(HALF)
    m = np.arange(1, 128)
    gap = np.mod(u[None, :] - 2 * n[:, None], TILE)
    line = (1.0 + 2.0 * np.cos(2.0 * np.pi * m[None, :] * u[:, None] / TILE).sum(1)) / HALF
    spread = line[gap]
    spread[:, 0::2] = np.eye(HALF)
    out = {}
    out["cs"] = split(cs)[0]
    out["pairs_hi"], out["pairs_lo"] = split(cs[0::2] + cs[1::2])
    out["even_t"] = split(cs[0::2].T)[0]
    edge = np.zeros((16, 256))
    edge[:4] = cs[[0, 1, TILE - 2, TILE - 1]]
    out["edge"] = split(edge)[0]
    out["spread"] = np.concatenate(split(spread), 0)
    return out


def dot(a, b):
    return lax.dot_general(a, b, (((1,), (0,)), ((), ())), preferred_element_type=F32)


def dot_nt(a, b):
    return lax.dot_general(a, b, (((1,), (1,)), ((), ())), preferred_element_type=F32)


def dot_tn(a, b):
    return lax.dot_general(a, b, (((0,), (0,)), ((), ())), preferred_element_type=F32)


def iota(shape, dim):
    return lax.broadcasted_iota(jnp.int32, shape, dim)


def fetch(sem, *pairs):
    copies = [pltpu.make_async_copy(src, dst, sem.at[i]) for i, (src, dst) in enumerate(pairs)]
    for copy in copies:
        copy.start()
    return copies


def picker(band_ref):
    band = band_ref[...]
    return (iota((256, 128), 0) == jnp.concatenate([band, band + 128], 1)).astype(BF)


def columns():
    row = iota((16, TILE), 0)
    col = jnp.where(row < 2, row, row + TILE - 4)
    return ((iota((16, TILE), 1) == col) & (row < 4)).astype(BF)


def strip_kernel(mask_in, quen_in, out_ref, mask, head, tail, edge, sem):
    copies = fetch(
        sem, *[(mask_in.at[:, pl.ds(128 * c, 128)], mask.at[c]) for c in range(4)],
        (quen_in.at[:, pl.ds(0, 8), :], head), (quen_in.at[:, pl.ds(STRIP - 8, 8), :], tail),
    )
    halves = (iota((TILE, HALF), 0) == 2 * iota((TILE, HALF), 1)).astype(BF)
    for copy in copies[:4]:
        copy.wait()
    rows = [mask[c, pl.ds(0, STRIP // 2, stride=2), :] for c in range(4)]
    coarse = dot(jnp.concatenate(rows, 1).astype(F32).astype(BF), halves).astype(BF)
    for copy in copies[4:]:
        copy.wait()
    for peer in range(8):
        out_ref[peer, 0:32, :] = coarse[:, 0:128]
        out_ref[peer, 32:64, :] = coarse[:, 128:256]
        for k, c in enumerate((0, 2, 1, 3)):
            edge[peer, 4 * k : 4 * k + 2, :] = head[peer, 0:2, 128 * c : 128 * (c + 1)]
            edge[peer, 4 * k + 2 : 4 * k + 4, :] = tail[peer, 6:8, 128 * c : 128 * (c + 1)]
        out_ref[peer, 64:80, :] = edge[peer].astype(BF)


def table_kernel(
    after, bx_in, by_in, cs_in, hi_in, lo_in, even_in, edge_in, quen_in, w_in,
    rows_ref, xhi_ref, xlo_ref, yhi_ref, ylo_ref, cols_ref, placed_ref, left_ref, right_ref, weight_ref,
    bx, by, cs, hi_tab, lo_tab, even, edge, quen, w, sem,
):
    copies = fetch(
        sem, (bx_in, bx), (by_in, by), (edge_in, edge), (even_in, even), (cs_in, cs), (hi_in, hi_tab), (lo_in, lo_tab),
        (w_in, w), (quen_in, quen),
    )
    for copy in copies[:8]:
        copy.wait()
    pick_x = picker(bx)
    pick_y = picker(by)
    rows_ref[...] = dot(cs[...], pick_x).astype(BF)
    xhi_ref[...] = dot(hi_tab[...], pick_x).T.astype(BF)
    xlo_ref[...] = dot(lo_tab[...], pick_x).T.astype(BF)
    yhi_ref[...] = dot(hi_tab[...], pick_y).astype(BF)
    ylo_ref[...] = dot(lo_tab[...], pick_y).astype(BF)
    table = dot_tn(pick_y, even[...])
    flip = jnp.where(iota((128, 1), 0) < BAND, 1.0, -1.0).astype(F32)
    cols_ref[:, 0:HALF] = (table * flip).astype(BF)
    cols_ref[:, HALF:TILE] = jnp.concatenate([table[BAND:], table[:BAND]], 0).astype(BF)
    sign = jnp.where(iota((1, 128), 1) < BAND, 1.0, -1.0).astype(F32)
    ends = dot(edge[...], pick_y)[0:8]
    ends = jnp.where(iota((8, 128), 0) < 4, sign * ends, pltpu.roll(pltpu.roll(ends, BAND, 1), 4, 0))
    count = placed_ref.shape[1] // 128
    own = iota((128, 128), 0) >> 3
    many = jnp.tile(ends, (16, 1))
    for k in range(count):
        placed_ref[:, 128 * k : 128 * (k + 1)] = jnp.where(own == k, many, 0.0).astype(BF)
        weight_ref[k : k + 1, :] = jnp.full((1, HALF), w[k], F32)
    copies[8].wait()
    ends = dot_nt(columns(), quen[...].reshape(PLANES * STRIP, TILE).astype(BF))
    for low, ref in ((0, left_ref), (2, right_ref)):
        ref[...] = jnp.zeros((16, 128), F32)
        for z in range(PLANES):
            ref[2 * z : 2 * z + 2, 0:STRIP] = ends[low : low + 2, STRIP * z : STRIP * (z + 1)]


def spectrum_kernel(
    w_ref, got_ref, kern_ref, rows_ref, xhi_ref, xlo_ref, yhi_ref, ylo_ref, placed_ref, qleft_ref, qright_ref,
    big_ref, left_ref, right_ref, ring_ref,
):
    lane = iota((1, 128), 1)
    sign = jnp.where(lane < BAND, -1.0, 1.0).astype(F32)
    coarse = jnp.concatenate([got_ref[:, 0:32, :].reshape(256, 128), got_ref[:, 32:64, :].reshape(256, 128)], 1)
    summed = dot(coarse, yhi_ref[...]) + dot(coarse, ylo_ref[...])
    hi = summed.astype(BF)
    lo = (summed - hi.astype(F32)).astype(BF)
    u = (dot(xhi_ref[...], hi) + dot(xhi_ref[...], lo) + dot(xlo_ref[...], hi)) * (1.0 / (TILE * TILE))
    v = u[:BAND] + sign * pltpu.roll(u[BAND:], BAND, 1)
    v_swap = pltpu.roll(v, BAND, 1)
    coef_a = jnp.where(lane < BAND, v, v_swap)
    coef_b = jnp.where(lane < BAND, v_swap, -v)
    count = kern_ref.shape[0]
    for k in range(count):
        cur = kern_ref[k].astype(F32)
        top = cur * coef_a + pltpu.roll(cur, BAND, 1) * coef_b
        big_ref[0:BAND, 128 * k : 128 * (k + 1)] = top.astype(BF)
        big_ref[BAND:128, 128 * k : 128 * (k + 1)] = (sign * pltpu.roll(top, BAND, 1)).astype(BF)
    narrow = dot_nt(placed_ref[...], big_ref[...]).astype(BF)
    field = dot_nt(narrow, rows_ref[...])
    total = jnp.zeros((8, TILE), F32)
    for k in range(count):
        part = field[8 * k : 8 * (k + 1)]
        total = total + w_ref[k : k + 1, 0:1] * (part * part)
    bright = total + pltpu.roll(total, 4, 0)
    place = iota((16, TILE), 0)
    eight = jnp.concatenate([bright, bright], 0)
    left_ref[:, 0:TILE] = jnp.where(place < 2, eight, 0.0).astype(BF)
    right_ref[:, 0:TILE] = jnp.where(place < 2, pltpu.roll(eight, 14, 0), 0.0).astype(BF)
    beyond = (iota((16, 128), 0) & 3) < 2
    heard = [got_ref[p, 64:80, :].astype(F32) for p in range(8)]
    rings = [jnp.where(beyond, heard[(p + 1) % 8], heard[(p + 7) % 8]) for p in range(8)]
    for p in range(8):
        ring_ref[p, :, 0:128] = rings[p][0:8]
        ring_ref[p, :, 128:HALF] = rings[p][8:16]
    row, col = iota((16, 128), 0), iota((16, 128), 1)
    for j, (ref, cols) in enumerate(((left_ref, qleft_ref), (right_ref, qright_ref))):
        pick = ((col == row + 126 * j) & (row < 2)).astype(BF)
        ends = dot_nt(pick, jnp.concatenate([ring[8 * j : 8 * j + 8] for ring in rings], 0).astype(BF))
        both = jnp.concatenate([ends, ends], 1)
        both = both if j == 0 else pltpu.roll(both, 124, 1)
        ref[:, TILE:WIDE] = jnp.where(col < STRIP, cols[...], both).astype(BF)


def image_kernel(w_ref, big_ref, rows_ref, cols_ref, img_ref):
    count = big_ref.shape[1] // 128
    chunk = 256
    cols = cols_ref[...]
    for part in range(TILE // chunk):
        half = dot(rows_ref[part * chunk : (part + 1) * chunk, :], big_ref[...]).astype(BF)
        total = jnp.zeros((chunk, HALF), F32)
        for k in range(count):
            field = dot(half[:, 128 * k : 128 * (k + 1)], cols)
            total = total + w_ref[k : k + 1, :] * (field[:, :HALF] * field[:, :HALF] + field[:, HALF:] * field[:, HALF:])
        img_ref[part * chunk : (part + 1) * chunk, :] = total


def pack_kernel(img_ref, ring_ref, from_left, from_right, out_ref, scr_ref):
    place = iota((8, WIDE), 0)
    far, near = from_left[...].astype(F32)[0:8], from_right[...].astype(F32)[0:8]
    both = jnp.where(place < 2, far, pltpu.roll(near, 2, 0))
    ends, both = both[:, TILE:WIDE], both[:, 0:TILE]
    lane = iota((8, 128), 1)
    for p in range(8):
        base = p * STRIP
        out_ref[p, 0:STRIP, :] = img_ref[base : base + STRIP, :].astype(BF)
        nxt = (base + STRIP) % TILE
        scr_ref[0:2, :] = img_ref[nxt : nxt + 2, :]
        prv = (base - 2) % TILE
        scr_ref[6:8, :] = img_ref[prv : prv + 2, :]
        first = pltpu.roll(both, (TILE - base) % TILE, 1)[:, 0:128]
        second = pltpu.roll(both, (TILE - base + CYC) % TILE, 1)[:, 0:128]
        side = jnp.where(lane < 66, first, jnp.where(lane < CYC, second, 0.0))
        scr_ref[2:6, 0:128] = side[0:4]
        first = pltpu.roll(ends, (128 - 8 * p) % 128, 1)
        second = pltpu.roll(ends, (132 - 8 * p) % 128, 1)
        scr_ref[2:6, 128:HALF] = jnp.where(lane < 66, first, second)[0:4]
        scr_ref[8:16, :] = ring_ref[p]
        out_ref[p, STRIP:80, :] = scr_ref[...].astype(BF)


def acid_side(got_ref):
    return got_ref[:, 64:80, 0:128].astype(F32).reshape(16 * PLANES, 128).T


def acid_cols(side, z):
    return pltpu.roll(side, (124 - 16 * z) % 128, 1)


def quen_side(from_left, from_right):
    both = [from_left[:, TILE:WIDE].astype(F32), from_right[:, TILE:WIDE].astype(F32), jnp.zeros((96, 128), F32)]
    return jnp.concatenate(both, 0).T


def quen_cols(side, z):
    behind = iota((1, 128), 1) >= STRIP
    return jnp.where(behind, pltpu.roll(side, (126 - 2 * z) % 128, 1), pltpu.roll(side, (112 - 2 * z) % 128, 1))


def quen_corner(got_ref):
    return got_ref[:, 64:80, 128:HALF].astype(F32).reshape(16 * PLANES, 128).T[STRIP:CYC]


def exposed(intensity):
    return 1.0 - jnp.exp(-DILL_RATE * intensity)


def edge_kernel(after, got_ref, spread_ref, m_ref, scr):
    last = lax.axis_index("depth") == 7
    coarse = got_ref[:, 64:80, :].reshape(16 * PLANES, HALF)
    fine = exposed(dot(jnp.concatenate([coarse, coarse], 1), spread_ref[...]))
    side = exposed(acid_side(got_ref)[STRIP:CYC])
    corner = quen_corner(got_ref)
    for z in range(PLANES):
        back = fine[16 * z : 16 * z + 8]
        outer = acid_cols(side, z)
        ring = got_ref[z, 64:80, :].astype(F32)
        end = acid_cols(corner, z)
        place = slice(2 * z, 2 * z + 2)
        scr[place, 0:TILE] = jnp.where(last, back[0:2], back[6:8])
        scr[place, TILE:WIDE] = jnp.where(last, outer[0:2], outer[6:8])
        place = slice(16 + 2 * z, 18 + 2 * z)
        scr[place, 0:HALF] = jnp.where(last, ring[8:10], ring[10:12])
        scr[place, HALF:TILE] = jnp.where(last, ring[12:14], ring[14:16])
        scr[place, TILE:WIDE] = jnp.where(last, end[0:2], end[6:8])
    m_ref[...] = scr[...].astype(BF)


def moved(src_a, src_q, z, t, cols):
    tiles, width = src_a.shape[1] // 8, src_a.shape[2]
    here, before, after = (pl.ds(8 * (i % tiles), 8) for i in (t, t - 1, t + 1))
    row = iota((8, 1), 0)
    a = src_a[z, here, 0:cols]
    q = src_q[z, here, 0:cols]
    react = REACT_RATE * a * q

    def move(c, ref, lat, vert):
        up = ref[min(z + 1, PLANES - 1), here, 0:cols]
        down = ref[max(z - 1, 0), here, 0:cols]
        wide = ref[z, here, :]
        near = pltpu.roll(jnp.where(row == 7, ref[z, before, 0:cols], c), 1, 0)
        near = near + pltpu.roll(jnp.where(row == 0, ref[z, after, 0:cols], c), 7, 0)
        near = near + (pltpu.roll(wide, 1, 1)[:, 0:cols] + pltpu.roll(wide, width - 1, 1)[:, 0:cols])
        return (1.0 - 4.0 * lat - 2.0 * vert) * c + lat * near + vert * (up + down) - react

    return move(a, src_a, ACID_LAT, ACID_VERT), move(q, src_q, QUEN_LAT, QUEN_VERT)


def bake_kernel(
    turn, got_ref, spread_ref, quen_ref, from_left, from_right, *refs,
):
    a_out, q_out, rim_ref, tile_ref, a_ref, q_ref, a_mid, q_mid, a_end, q_end, sem = refs[-11:]

    @pl.when((lax.axis_index("tx") & 1) == turn)
    def _():
        side = exposed(acid_side(got_ref)[0:CYC])
        side_q = quen_side(from_left, from_right)[0:STRIP]
        corner = quen_corner(got_ref)
        coarse = got_ref[...].reshape(PLANES * 80, HALF)
        fine = dot(jnp.concatenate([coarse, coarse], 1), spread_ref[...])
        for z in range(PLANES):
            a_ref[z, :, 0:TILE] = exposed(fine[80 * z : 80 * z + CYC])
            a_ref[z, :, TILE:WIDE] = acid_cols(side, z)
            q_ref[z, 0:STRIP, 0:TILE] = quen_ref[z]
            q_ref[z, 0:STRIP, TILE:WIDE] = quen_cols(side_q, z)
            ring = got_ref[z, STRIP:80, :].astype(F32)
            q_ref[z, STRIP:CYC, 0:TILE] = jnp.zeros((8, TILE), F32)
            q_ref[z, STRIP:CYC, TILE:WIDE] = acid_cols(corner, z)
            for i, row in ((0, STRIP), (2, 70)):
                q_ref[z, row : row + 2, 0:HALF] = ring[8 + i : 10 + i]
                q_ref[z, row : row + 2, HALF:TILE] = ring[12 + i : 14 + i]
        for z in range(PLANES):
            for t in range(CYC // 8):
                spot = pl.ds(8 * t, 8)
                a_mid[z, spot, :], q_mid[z, spot, :] = moved(a_ref, q_ref, z, t, WIDE)
        copies = []
        for z in range(PLANES):
            for t in range(STRIP // 8):
                spot = pl.ds(8 * t, 8)
                a_end[z, spot, :], q_end[z, spot, :] = moved(a_mid, q_mid, z, t, TILE)
            for i, (src, dst) in enumerate(((a_end, a_out), (q_end, q_out))):
                copies.append(pltpu.make_async_copy(src.at[z], dst.at[z], sem.at[i, z]))
                copies[-1].start()
        level = lax.axis_index("depth")
        for edge, start in ((0, 0), (7, STRIP - 8)):

            @pl.when(level == edge)
            def _():
                rim_ref[0] = a_end[:, start : start + 8, :]
                rim_ref[1] = q_end[:, start : start + 8, :]
                tile_ref[0] = a_ref[:, start : start + 8, :]
                tile_ref[1] = q_ref[:, start : start + 8, :]

        for copy in copies:
            copy.wait()


def patch_kernel(m_ref, rim_even, tile_even, rim_odd, tile_odd, a_in, q_in, a_out, q_out, a_ref, q_ref, a_mid, q_mid, a_end, q_end, sem):
    level = lax.axis_index("depth")
    last = level == 7

    @pl.when((level == 0) | last)
    def _():
        spot = pl.ds(pl.multiple_of(jnp.where(last, STRIP - 8, 0), 8), 8)
        row = iota((8, 1), 0)
        heard = jnp.where(last, row - 2, 5 - row) < 0
        mine = jnp.where(last, row - 6, 1 - row) >= 0
        m = m_ref[...].astype(F32)
        odd = (lax.axis_index("tx") & 1) == 1
        for z in range(PLANES):
            for f, ref in ((0, a_ref), (1, q_ref)):
                pair = m[16 * f + 2 * z : 16 * f + 2 * z + 2]
                ref[z] = jnp.where(heard, jnp.concatenate([pair] * 4, 0), jnp.where(odd, tile_odd[f, z], tile_even[f, z]))
        for z in range(PLANES):
            a_mid[z], q_mid[z] = moved(a_ref, q_ref, z, 0, WIDE)
        for z in range(PLANES):
            a, q = moved(a_mid, q_mid, z, 0, TILE)
            a_end[z] = jnp.where(mine, a, jnp.where(odd, rim_odd[0, z], rim_even[0, z]))
            q_end[z] = jnp.where(mine, q, jnp.where(odd, rim_odd[1, z], rim_even[1, z]))
        for copy in fetch(sem, (a_end, a_out.at[:, spot, :]), (q_end, q_out.at[:, spot, :])):
            copy.wait()


ANY = pl.BlockSpec(memory_space=pl.ANY)
HBM = pl.BlockSpec(memory_space=pltpu.HBM)


def call(kernel, out, specs, scratch=(), outs=None, flops=0, size=0, limit=LIMIT, **more):
    return pl.pallas_call(
        kernel,
        out_shape=out,
        in_specs=specs,
        out_specs=jax.tree.map(lambda _: VMEM, out) if outs is None else outs,
        scratch_shapes=scratch,
        compiler_params=pltpu.CompilerParams(vmem_limit_bytes=limit),
        cost_estimate=pl.CostEstimate(flops=flops, bytes_accessed=size, transcendentals=0),
        **more,
    )


def on_device(sizes, mask, kernels, weights, band_rows, band_cols, quencher):
    n_depth, n_tx, n_ty = sizes
    con = constants()
    count = kernels.shape[1]
    shape = jax.ShapeDtypeStruct
    dma = pltpu.SemaphoreType.DMA
    bx = band_rows.reshape(1, BAND)
    by = band_cols.reshape(1, BAND)
    quen = quencher[:, 0]
    table = pltpu.VMEM((256, 256), BF)
    band = pltpu.VMEM((1, BAND), jnp.int32)

    packed = call(
        strip_kernel, shape((8, 80, 128), BF), [HBM] * 2, limit=MOST,
        scratch=[
            pltpu.VMEM((4, STRIP, 128), jnp.int32), pltpu.VMEM((PLANES, 8, TILE), F32),
            pltpu.VMEM((PLANES, 8, TILE), F32), pltpu.VMEM((8, 16, 128), F32), dma((6,)),
        ],
    )(mask[0], quen)
    got = lax.all_to_all(packed, "depth", 0, 0, tiled=True)
    *tables, cols, placed, qleft, qright, weight = call(
        table_kernel,
        (
            shape((TILE, 128), BF), *[shape((128, 256), BF)] * 2, *[shape((256, 128), BF)] * 2, shape((128, TILE), BF),
            shape((128, 128 * count), BF), shape((16, 128), F32), shape((16, 128), F32), shape((16, HALF), F32),
        ),
        [ANY] + [HBM] * 9,
        scratch=[
            band, band, pltpu.VMEM((TILE, 256), BF), table, table, table, pltpu.VMEM((16, 256), BF),
            pltpu.VMEM((PLANES, STRIP, TILE), F32), pltpu.SMEM((count,), F32), dma((9,)),
        ],
        flops=400_000_000, size=2_000_000,
    )(packed, bx, by, con["cs"], con["pairs_hi"], con["pairs_lo"], con["even_t"], con["edge"], quen, weights)
    rows = tables[0]
    big, left, right, ring = call(
        spectrum_kernel,
        (
            shape((128, 128 * count), BF), shape((16, WIDE), BF), shape((16, WIDE), BF),
            shape((8, 8, HALF), F32),
        ),
        [VMEM] * 11,
    )(weight, got, kernels[0], *tables, placed, qleft, qright)
    from_right = lax.ppermute(left, "ty", [(i, (i - 1) % n_ty) for i in range(n_ty)])
    from_left = lax.ppermute(right, "ty", [(i, (i + 1) % n_ty) for i in range(n_ty)])
    image = call(
        image_kernel, shape((TILE, HALF), F32), [VMEM] * 4, flops=2_400_000_000, size=2_000_000,
    )(weight, big, rows, cols)
    strips = call(
        pack_kernel, shape((8, 80, HALF), BF), [VMEM] * 4, scratch=[pltpu.VMEM((16, HALF), F32)],
    )(image, ring, from_left, from_right)
    planes = lax.all_to_all(strips, "depth", 0, 0, tiled=True)
    tile = pltpu.VMEM((PLANES, 8, TILE), F32)
    out = shape((PLANES, STRIP, TILE), F32)
    wide = pltpu.VMEM((PLANES, CYC, WIDE), F32)
    done = pltpu.VMEM((PLANES, STRIP, TILE), F32)

    def bake(turn, *before):
        return call(
            functools.partial(bake_kernel, turn), (out, out, shape((2, PLANES, 8, TILE), F32), shape((2, PLANES, 8, WIDE), F32)),
            [VMEM] * 5 + [HBM] * len(before), outs=(HBM, HBM, VMEM, VMEM),
            scratch=[wide, wide, wide, wide, done, done, dma((2, PLANES))], flops=3_000_000_000, size=4_000_000,
            input_output_aliases={5 + i: i for i in range(len(before))},
        )(planes, con["spread"], quen, from_left, from_right, *before)

    acid, left_over, *odd = bake(1)
    outer = call(
        edge_kernel, shape((32, WIDE), BF), [ANY] + [VMEM] * 2, scratch=[pltpu.VMEM((32, WIDE), F32)],
    )(odd[0], planes, con["spread"])
    end = (n_depth - 1) * n_tx
    pairs = [(t, (t + 1) % n_tx) for t in range(n_tx)] + [(end + t, end + (t - 1) % n_tx) for t in range(n_tx)]
    outer = lax.ppermute(outer, ("depth", "tx"), pairs)
    acid, left_over, *even = bake(0, acid, left_over)
    low = pltpu.VMEM((PLANES, 8, WIDE), F32)
    acid, left_over = call(
        patch_kernel, (out, out), [VMEM] * 5 + [HBM] * 2, outs=(HBM, HBM),
        scratch=[low, low, low, low, tile, tile, dma((2,))], input_output_aliases={5: 0, 6: 1},
    )(outer, *even, *odd, acid, left_over)
    return acid[:, None], left_over[:, None]


def solution(mesh):
    sizes = (mesh.shape["depth"], mesh.shape["tx"], mesh.shape["ty"])
    placed = (
        P("tx", "depth", "ty"),
        P("depth", None, None, None),
        P(),
        P(),
        P(),
        P(None, "tx", "depth", "ty"),
    )
    return jax.shard_map(
        functools.partial(on_device, sizes),
        mesh=mesh,
        in_specs=placed,
        out_specs=(P(None, "tx", "depth", "ty"), P(None, "tx", "depth", "ty")),
        check_vma=False,
    )
```

```python
import functools
import math

import jax
import jax.numpy as jnp
import numpy as np
from jax import lax
from jax.experimental import pallas as pl
from jax.experimental.pallas import tpu as pltpu
from jax.sharding import PartitionSpec as P

BF = jnp.bfloat16
F32 = jnp.float32
TILE = 512
BAND = 64
HALF = 256
PLANES = 8
STRIP = 64
CYC = 72
WIDE = 640
DILL_RATE = 1.0
REACT_RATE = 0.4
ACID_LAT, ACID_VERT = 0.23, 0.03
QUEN_LAT, QUEN_VERT = 0.15, 0.05
VMEM = pl.BlockSpec(memory_space=pltpu.VMEM)
SMEM = pl.BlockSpec(memory_space=pltpu.SMEM)
LIMIT = 40 * 1024 * 1024
MOST = 60 * 1024 * 1024


def split(x):
    hi = np.asarray(x, np.float32).astype(jnp.bfloat16)
    lo = (np.asarray(x, np.float64) - hi.astype(np.float64)).astype(np.float32).astype(jnp.bfloat16)
    return hi, lo


@functools.cache
def constants():
    u = np.arange(TILE)
    f = np.arange(128) - BAND // 2
    angle = np.mod(u[:, None] * f[None, :], TILE) * (2.0 * np.pi / TILE)
    cs = np.concatenate([np.cos(angle), np.sin(angle)], 1)
    n = np.arange(HALF)
    m = np.arange(1, 128)
    gap = np.mod(u[None, :] - 2 * n[:, None], TILE)
    line = (1.0 + 2.0 * np.cos(2.0 * np.pi * m[None, :] * u[:, None] / TILE).sum(1)) / HALF
    spread = line[gap]
    spread[:, 0::2] = np.eye(HALF)
    out = {}
    out["cs"] = split(cs)[0]
    out["pairs_hi"], out["pairs_lo"] = split(cs[0::2] + cs[1::2])
    out["even_t"] = split(cs[0::2].T)[0]
    edge = np.zeros((16, 256))
    edge[:4] = cs[[0, 1, TILE - 2, TILE - 1]]
    out["edge"] = split(edge)[0]
    out["spread"] = np.concatenate(split(spread), 0)
    return out


def dot(a, b):
    return lax.dot_general(a, b, (((1,), (0,)), ((), ())), preferred_element_type=F32)


def dot_nt(a, b):
    return lax.dot_general(a, b, (((1,), (1,)), ((), ())), preferred_element_type=F32)


def dot_tn(a, b):
    return lax.dot_general(a, b, (((0,), (0,)), ((), ())), preferred_element_type=F32)


def iota(shape, dim):
    return lax.broadcasted_iota(jnp.int32, shape, dim)


def fetch(sem, *pairs):
    copies = [pltpu.make_async_copy(src, dst, sem.at[i]) for i, (src, dst) in enumerate(pairs)]
    for copy in copies:
        copy.start()
    return copies


def picker(band_ref):
    band = band_ref[...]
    return (iota((256, 128), 0) == jnp.concatenate([band, band + 128], 1)).astype(BF)


def columns():
    row = iota((16, TILE), 0)
    col = jnp.where(row < 2, row, row + TILE - 4)
    return ((iota((16, TILE), 1) == col) & (row < 4)).astype(BF)


def strip_kernel(mask_in, quen_in, out_ref, mask, head, tail, edge, sem):
    copies = fetch(
        sem, *[(mask_in.at[:, pl.ds(128 * c, 128)], mask.at[c]) for c in range(4)],
        (quen_in.at[:, pl.ds(0, 8), :], head), (quen_in.at[:, pl.ds(STRIP - 8, 8), :], tail),
    )
    halves = (iota((TILE, HALF), 0) == 2 * iota((TILE, HALF), 1)).astype(BF)
    for copy in copies[:4]:
        copy.wait()
    rows = [mask[c, pl.ds(0, STRIP // 2, stride=2), :] for c in range(4)]
    coarse = dot(jnp.concatenate(rows, 1).astype(F32).astype(BF), halves).astype(BF)
    for copy in copies[4:]:
        copy.wait()
    for peer in range(8):
        out_ref[peer, 0:32, :] = coarse[:, 0:128]
        out_ref[peer, 32:64, :] = coarse[:, 128:256]
        for k, c in enumerate((0, 2, 1, 3)):
            edge[peer, 4 * k : 4 * k + 2, :] = head[peer, 0:2, 128 * c : 128 * (c + 1)]
            edge[peer, 4 * k + 2 : 4 * k + 4, :] = tail[peer, 6:8, 128 * c : 128 * (c + 1)]
        out_ref[peer, 64:80, :] = edge[peer].astype(BF)


def table_kernel(
    after, bx_in, by_in, cs_in, hi_in, lo_in, even_in, edge_in, quen_in, w_in,
    rows_ref, xhi_ref, xlo_ref, yhi_ref, ylo_ref, cols_ref, placed_ref, left_ref, right_ref, weight_ref,
    bx, by, cs, hi_tab, lo_tab, even, edge, quen, w, sem,
):
    copies = fetch(
        sem, (bx_in, bx), (by_in, by), (edge_in, edge), (even_in, even), (cs_in, cs), (hi_in, hi_tab), (lo_in, lo_tab),
        (w_in, w), (quen_in, quen),
    )
    for copy in copies[:8]:
        copy.wait()
    pick_x = picker(bx)
    pick_y = picker(by)
    rows_ref[...] = dot(cs[...], pick_x).astype(BF)
    xhi_ref[...] = dot(hi_tab[...], pick_x).T.astype(BF)
    xlo_ref[...] = dot(lo_tab[...], pick_x).T.astype(BF)
    yhi_ref[...] = dot(hi_tab[...], pick_y).astype(BF)
    ylo_ref[...] = dot(lo_tab[...], pick_y).astype(BF)
    table = dot_tn(pick_y, even[...])
    flip = jnp.where(iota((128, 1), 0) < BAND, 1.0, -1.0).astype(F32)
    cols_ref[:, 0:HALF] = (table * flip).astype(BF)
    cols_ref[:, HALF:TILE] = jnp.concatenate([table[BAND:], table[:BAND]], 0).astype(BF)
    sign = jnp.where(iota((1, 128), 1) < BAND, 1.0, -1.0).astype(F32)
    ends = dot(edge[...], pick_y)[0:8]
    ends = jnp.where(iota((8, 128), 0) < 4, sign * ends, pltpu.roll(pltpu.roll(ends, BAND, 1), 4, 0))
    count = placed_ref.shape[1] // 128
    own = iota((128, 128), 0) >> 3
    many = jnp.tile(ends, (16, 1))
    for k in range(count):
        placed_ref[:, 128 * k : 128 * (k + 1)] = jnp.where(own == k, many, 0.0).astype(BF)
        weight_ref[k : k + 1, :] = jnp.full((1, HALF), w[k], F32)
    copies[8].wait()
    ends = dot_nt(columns(), quen[...].reshape(PLANES * STRIP, TILE).astype(BF))
    for low, ref in ((0, left_ref), (2, right_ref)):
        ref[...] = jnp.zeros((16, 128), F32)
        for z in range(PLANES):
            ref[2 * z : 2 * z + 2, 0:STRIP] = ends[low : low + 2, STRIP * z : STRIP * (z + 1)]


def spectrum_kernel(
    w_ref, got_ref, kern_ref, rows_ref, xhi_ref, xlo_ref, yhi_ref, ylo_ref, placed_ref, qleft_ref, qright_ref,
    big_ref, left_ref, right_ref, ring_ref,
):
    lane = iota((1, 128), 1)
    sign = jnp.where(lane < BAND, -1.0, 1.0).astype(F32)
    coarse = jnp.concatenate([got_ref[:, 0:32, :].reshape(256, 128), got_ref[:, 32:64, :].reshape(256, 128)], 1)
    summed = dot(coarse, yhi_ref[...]) + dot(coarse, ylo_ref[...])
    hi = summed.astype(BF)
    lo = (summed - hi.astype(F32)).astype(BF)
    u = (dot(xhi_ref[...], hi) + dot(xhi_ref[...], lo) + dot(xlo_ref[...], hi)) * (1.0 / (TILE * TILE))
    v = u[:BAND] + sign * pltpu.roll(u[BAND:], BAND, 1)
    v_swap = pltpu.roll(v, BAND, 1)
    coef_a = jnp.where(lane < BAND, v, v_swap)
    coef_b = jnp.where(lane < BAND, v_swap, -v)
    count = kern_ref.shape[0]
    for k in range(count):
        cur = kern_ref[k].astype(F32)
        top = cur * coef_a + pltpu.roll(cur, BAND, 1) * coef_b
        big_ref[0:BAND, 128 * k : 128 * (k + 1)] = top.astype(BF)
        big_ref[BAND:128, 128 * k : 128 * (k + 1)] = (sign * pltpu.roll(top, BAND, 1)).astype(BF)
    narrow = dot_nt(placed_ref[...], big_ref[...]).astype(BF)
    field = dot_nt(narrow, rows_ref[...])
    total = jnp.zeros((8, TILE), F32)
    for k in range(count):
        part = field[8 * k : 8 * (k + 1)]
        total = total + w_ref[k : k + 1, 0:1] * (part * part)
    bright = total + pltpu.roll(total, 4, 0)
    place = iota((16, TILE), 0)
    eight = jnp.concatenate([bright, bright], 0)
    left_ref[:, 0:TILE] = jnp.where(place < 2, eight, 0.0).astype(BF)
    right_ref[:, 0:TILE] = jnp.where(place < 2, pltpu.roll(eight, 14, 0), 0.0).astype(BF)
    beyond = (iota((16, 128), 0) & 3) < 2
    heard = [got_ref[p, 64:80, :].astype(F32) for p in range(8)]
    rings = [jnp.where(beyond, heard[(p + 1) % 8], heard[(p + 7) % 8]) for p in range(8)]
    for p in range(8):
        ring_ref[p, :, 0:128] = rings[p][0:8]
        ring_ref[p, :, 128:HALF] = rings[p][8:16]
    row, col = iota((16, 128), 0), iota((16, 128), 1)
    for j, (ref, cols) in enumerate(((left_ref, qleft_ref), (right_ref, qright_ref))):
        pick = ((col == row + 126 * j) & (row < 2)).astype(BF)
        ends = dot_nt(pick, jnp.concatenate([ring[8 * j : 8 * j + 8] for ring in rings], 0).astype(BF))
        both = jnp.concatenate([ends, ends], 1)
        both = both if j == 0 else pltpu.roll(both, 124, 1)
        ref[:, TILE:WIDE] = jnp.where(col < STRIP, cols[...], both).astype(BF)


def image_kernel(w_ref, big_ref, rows_ref, cols_ref, img_ref):
    count = big_ref.shape[1] // 128
    chunk = 256
    cols = cols_ref[...]
    for part in range(TILE // chunk):
        half = dot(rows_ref[part * chunk : (part + 1) * chunk, :], big_ref[...]).astype(BF)
        total = jnp.zeros((chunk, HALF), F32)
        for k in range(count):
            field = dot(half[:, 128 * k : 128 * (k + 1)], cols)
            total = total + w_ref[k : k + 1, :] * (field[:, :HALF] * field[:, :HALF] + field[:, HALF:] * field[:, HALF:])
        img_ref[part * chunk : (part + 1) * chunk, :] = total


def pack_kernel(img_ref, ring_ref, from_left, from_right, out_ref, scr_ref):
    place = iota((8, WIDE), 0)
    far, near = from_left[...].astype(F32)[0:8], from_right[...].astype(F32)[0:8]
    both = jnp.where(place < 2, far, pltpu.roll(near, 2, 0))
    ends, both = both[:, TILE:WIDE], both[:, 0:TILE]
    lane = iota((8, 128), 1)
    for p in range(8):
        base = p * STRIP
        out_ref[7 - p, 0:STRIP, :] = img_ref[base : base + STRIP, :].astype(BF)
        nxt = (base + STRIP) % TILE
        scr_ref[0:2, :] = img_ref[nxt : nxt + 2, :]
        prv = (base - 2) % TILE
        scr_ref[6:8, :] = img_ref[prv : prv + 2, :]
        first = pltpu.roll(both, (TILE - base) % TILE, 1)[:, 0:128]
        second = pltpu.roll(both, (TILE - base + CYC) % TILE, 1)[:, 0:128]
        side = jnp.where(lane < 66, first, jnp.where(lane < CYC, second, 0.0))
        scr_ref[2:6, 0:128] = side[0:4]
        first = pltpu.roll(ends, (128 - 8 * p) % 128, 1)
        second = pltpu.roll(ends, (132 - 8 * p) % 128, 1)
        scr_ref[2:6, 128:HALF] = jnp.where(lane < 66, first, second)[0:4]
        scr_ref[8:16, :] = ring_ref[p]
        out_ref[7 - p, STRIP:80, :] = scr_ref[...].astype(BF)


def acid_side(got_ref):
    return got_ref[:, 64:80, 0:128].astype(F32).reshape(16 * PLANES, 128).T


def acid_cols(side, z):
    return pltpu.roll(side, (12 + 16 * z) % 128, 1)


def quen_side(from_left, from_right):
    both = [from_left[:, TILE:WIDE].astype(F32), from_right[:, TILE:WIDE].astype(F32), jnp.zeros((96, 128), F32)]
    return jnp.concatenate(both, 0).T


def quen_cols(side, z):
    behind = iota((1, 128), 1) >= STRIP
    return jnp.where(behind, pltpu.roll(side, (126 - 2 * z) % 128, 1), pltpu.roll(side, (112 - 2 * z) % 128, 1))


def quen_corner(got_ref):
    return got_ref[:, 64:80, 128:HALF].astype(F32).reshape(16 * PLANES, 128).T[STRIP:CYC]


def exposed(intensity):
    return 1.0 - jnp.exp(-DILL_RATE * intensity)


def edge_kernel(after, got_ref, spread_ref, m_ref, scr):
    last = lax.axis_index("depth") == 7
    coarse = got_ref[:, 64:80, :].reshape(16 * PLANES, HALF)
    fine = exposed(dot(jnp.concatenate([coarse, coarse], 1), spread_ref[...]))
    side = exposed(acid_side(got_ref)[STRIP:CYC])
    corner = quen_corner(got_ref)
    for z in range(PLANES):
        seat = 7 - z
        back = fine[16 * seat : 16 * seat + 8]
        outer = acid_cols(side, z)
        ring = got_ref[seat, 64:80, :].astype(F32)
        end = acid_cols(corner, z)
        place = slice(2 * z, 2 * z + 2)
        scr[place, 0:TILE] = jnp.where(last, back[0:2], back[6:8])
        scr[place, TILE:WIDE] = jnp.where(last, outer[0:2], outer[6:8])
        place = slice(16 + 2 * z, 18 + 2 * z)
        scr[place, 0:HALF] = jnp.where(last, ring[8:10], ring[10:12])
        scr[place, HALF:TILE] = jnp.where(last, ring[12:14], ring[14:16])
        scr[place, TILE:WIDE] = jnp.where(last, end[0:2], end[6:8])
    m_ref[...] = scr[...].astype(BF)


def moved(src_a, src_q, z, t, cols):
    tiles, width = src_a.shape[1] // 8, src_a.shape[2]
    here, before, after = (pl.ds(8 * (i % tiles), 8) for i in (t, t - 1, t + 1))
    row = iota((8, 1), 0)
    a = src_a[z, here, 0:cols]
    q = src_q[z, here, 0:cols]
    react = REACT_RATE * a * q

    def move(c, ref, lat, vert):
        up = ref[min(z + 1, PLANES - 1), here, 0:cols]
        down = ref[max(z - 1, 0), here, 0:cols]
        wide = ref[z, here, :]
        near = pltpu.roll(jnp.where(row == 7, ref[z, before, 0:cols], c), 1, 0)
        near = near + pltpu.roll(jnp.where(row == 0, ref[z, after, 0:cols], c), 7, 0)
        near = near + (pltpu.roll(wide, 1, 1)[:, 0:cols] + pltpu.roll(wide, width - 1, 1)[:, 0:cols])
        return (1.0 - 4.0 * lat - 2.0 * vert) * c + lat * near + vert * (up + down) - react

    return move(a, src_a, ACID_LAT, ACID_VERT), move(q, src_q, QUEN_LAT, QUEN_VERT)


def bake_kernel(
    turn, got_ref, spread_ref, quen_ref, from_left, from_right, *refs,
):
    a_out, q_out, rim_ref, tile_ref, a_ref, q_ref, a_mid, q_mid, a_end, q_end, sem = refs[-11:]

    @pl.when((lax.axis_index("tx") & 1) == turn)
    def _():
        side = exposed(acid_side(got_ref)[0:CYC])
        side_q = quen_side(from_left, from_right)[0:STRIP]
        corner = quen_corner(got_ref)
        coarse = got_ref[...].reshape(PLANES * 80, HALF)
        fine = dot(jnp.concatenate([coarse, coarse], 1), spread_ref[...])
        for z in range(PLANES):
            seat = 7 - z
            a_ref[z, :, 0:TILE] = exposed(fine[80 * seat : 80 * seat + CYC])
            a_ref[z, :, TILE:WIDE] = acid_cols(side, z)
            q_ref[z, 0:STRIP, 0:TILE] = quen_ref[z]
            q_ref[z, 0:STRIP, TILE:WIDE] = quen_cols(side_q, z)
            ring = got_ref[seat, STRIP:80, :].astype(F32)
            q_ref[z, STRIP:CYC, 0:TILE] = jnp.zeros((8, TILE), F32)
            q_ref[z, STRIP:CYC, TILE:WIDE] = acid_cols(corner, z)
            for i, row in ((0, STRIP), (2, 70)):
                q_ref[z, row : row + 2, 0:HALF] = ring[8 + i : 10 + i]
                q_ref[z, row : row + 2, HALF:TILE] = ring[12 + i : 14 + i]
        for z in range(PLANES):
            for t in range(CYC // 8):
                spot = pl.ds(8 * t, 8)
                a_mid[z, spot, :], q_mid[z, spot, :] = moved(a_ref, q_ref, z, t, WIDE)
        copies = []
        for z in range(PLANES):
            for t in range(STRIP // 8):
                spot = pl.ds(8 * t, 8)
                a_end[z, spot, :], q_end[z, spot, :] = moved(a_mid, q_mid, z, t, TILE)
            for i, (src, dst) in enumerate(((a_end, a_out), (q_end, q_out))):
                copies.append(pltpu.make_async_copy(src.at[z], dst.at[z], sem.at[i, z]))
                copies[-1].start()
        level = lax.axis_index("depth")
        for edge, start in ((0, 0), (7, STRIP - 8)):

            @pl.when(level == edge)
            def _():
                rim_ref[0] = a_end[:, start : start + 8, :]
                rim_ref[1] = q_end[:, start : start + 8, :]
                tile_ref[0] = a_ref[:, start : start + 8, :]
                tile_ref[1] = q_ref[:, start : start + 8, :]

        for copy in copies:
            copy.wait()


def patch_kernel(m_ref, rim_even, tile_even, rim_odd, tile_odd, a_in, q_in, a_out, q_out, a_ref, q_ref, a_mid, q_mid, a_end, q_end, sem):
    level = lax.axis_index("depth")
    last = level == 7

    @pl.when((level == 0) | last)
    def _():
        spot = pl.ds(pl.multiple_of(jnp.where(last, STRIP - 8, 0), 8), 8)
        row = iota((8, 1), 0)
        heard = jnp.where(last, row - 2, 5 - row) < 0
        mine = jnp.where(last, row - 6, 1 - row) >= 0
        m = m_ref[...].astype(F32)
        odd = (lax.axis_index("tx") & 1) == 1
        for z in range(PLANES):
            for f, ref in ((0, a_ref), (1, q_ref)):
                pair = m[16 * f + 2 * z : 16 * f + 2 * z + 2]
                ref[z] = jnp.where(heard, jnp.concatenate([pair] * 4, 0), jnp.where(odd, tile_odd[f, z], tile_even[f, z]))
        for z in range(PLANES):
            a_mid[z], q_mid[z] = moved(a_ref, q_ref, z, 0, WIDE)
        for z in range(PLANES):
            a, q = moved(a_mid, q_mid, z, 0, TILE)
            a_end[z] = jnp.where(mine, a, jnp.where(odd, rim_odd[0, z], rim_even[0, z]))
            q_end[z] = jnp.where(mine, q, jnp.where(odd, rim_odd[1, z], rim_even[1, z]))
        for copy in fetch(sem, (a_end, a_out.at[:, spot, :]), (q_end, q_out.at[:, spot, :])):
            copy.wait()


ANY = pl.BlockSpec(memory_space=pl.ANY)
HBM = pl.BlockSpec(memory_space=pltpu.HBM)


def call(kernel, out, specs, scratch=(), outs=None, flops=0, size=0, limit=LIMIT, **more):
    return pl.pallas_call(
        kernel,
        out_shape=out,
        in_specs=specs,
        out_specs=jax.tree.map(lambda _: VMEM, out) if outs is None else outs,
        scratch_shapes=scratch,
        compiler_params=pltpu.CompilerParams(vmem_limit_bytes=limit),
        cost_estimate=pl.CostEstimate(flops=flops, bytes_accessed=size, transcendentals=0),
        **more,
    )


def on_device(sizes, mask, kernels, weights, band_rows, band_cols, quencher):
    n_depth, n_tx, n_ty = sizes
    con = constants()
    count = kernels.shape[1]
    shape = jax.ShapeDtypeStruct
    dma = pltpu.SemaphoreType.DMA
    bx = band_rows.reshape(1, BAND)
    by = band_cols.reshape(1, BAND)
    quen = quencher[:, 0]
    table = pltpu.VMEM((256, 256), BF)
    band = pltpu.VMEM((1, BAND), jnp.int32)

    packed = call(
        strip_kernel, shape((8, 80, 128), BF), [HBM] * 2, limit=MOST,
        scratch=[
            pltpu.VMEM((4, STRIP, 128), jnp.int32), pltpu.VMEM((PLANES, 8, TILE), F32),
            pltpu.VMEM((PLANES, 8, TILE), F32), pltpu.VMEM((8, 16, 128), F32), dma((6,)),
        ],
    )(mask[0], quen)
    got = lax.all_to_all(packed, "depth", 0, 0, tiled=True)
    *tables, cols, placed, qleft, qright, weight = call(
        table_kernel,
        (
            shape((TILE, 128), BF), *[shape((128, 256), BF)] * 2, *[shape((256, 128), BF)] * 2, shape((128, TILE), BF),
            shape((128, 128 * count), BF), shape((16, 128), F32), shape((16, 128), F32), shape((16, HALF), F32),
        ),
        [ANY] + [HBM] * 9,
        scratch=[
            band, band, pltpu.VMEM((TILE, 256), BF), table, table, table, pltpu.VMEM((16, 256), BF),
            pltpu.VMEM((PLANES, STRIP, TILE), F32), pltpu.SMEM((count,), F32), dma((9,)),
        ],
        flops=400_000_000, size=2_000_000,
    )(packed, bx, by, con["cs"], con["pairs_hi"], con["pairs_lo"], con["even_t"], con["edge"], quen, weights)
    rows = tables[0]
    big, left, right, ring = call(
        spectrum_kernel,
        (
            shape((128, 128 * count), BF), shape((16, WIDE), BF), shape((16, WIDE), BF),
            shape((8, 8, HALF), F32),
        ),
        [VMEM] * 11,
    )(weight, got, kernels[0], *tables, placed, qleft, qright)
    from_right = lax.ppermute(left, "ty", [(i, (i - 1) % n_ty) for i in range(n_ty)])
    from_left = lax.ppermute(right, "ty", [(i, (i + 1) % n_ty) for i in range(n_ty)])
    image = call(
        image_kernel, shape((TILE, HALF), F32), [VMEM] * 4, flops=2_400_000_000, size=2_000_000,
    )(weight, big, rows, cols)
    strips = call(
        pack_kernel, shape((8, 80, HALF), BF), [VMEM] * 4, scratch=[pltpu.VMEM((16, HALF), F32)],
    )(image, ring, from_left, from_right)
    seats = list(range(n_depth))[::-1]
    planes = lax.all_to_all(strips, "depth", 0, 0, tiled=True, axis_index_groups=[seats])
    tile = pltpu.VMEM((PLANES, 8, TILE), F32)
    out = shape((PLANES, STRIP, TILE), F32)
    wide = pltpu.VMEM((PLANES, CYC, WIDE), F32)
    done = pltpu.VMEM((PLANES, STRIP, TILE), F32)

    def bake(turn, *before):
        return call(
            functools.partial(bake_kernel, turn), (out, out, shape((2, PLANES, 8, TILE), F32), shape((2, PLANES, 8, WIDE), F32)),
            [VMEM] * 5 + [HBM] * len(before), outs=(HBM, HBM, VMEM, VMEM),
            scratch=[wide, wide, wide, wide, done, done, dma((2, PLANES))], flops=3_000_000_000, size=4_000_000,
            input_output_aliases={5 + i: i for i in range(len(before))},
        )(planes, con["spread"], quen, from_left, from_right, *before)

    acid, left_over, *odd = bake(1)
    outer = call(
        edge_kernel, shape((32, WIDE), BF), [ANY] + [VMEM] * 2, scratch=[pltpu.VMEM((32, WIDE), F32)],
    )(odd[0], planes, con["spread"])
    end = (n_depth - 1) * n_tx
    pairs = [(t, (t + 1) % n_tx) for t in range(n_tx)] + [(end + t, end + (t - 1) % n_tx) for t in range(n_tx)]
    outer = lax.ppermute(outer, ("depth", "tx"), pairs)
    acid, left_over, *even = bake(0, acid, left_over)
    low = pltpu.VMEM((PLANES, 8, WIDE), F32)
    acid, left_over = call(
        patch_kernel, (out, out), [VMEM] * 5 + [HBM] * 2, outs=(HBM, HBM),
        scratch=[low, low, low, low, tile, tile, dma((2,))], input_output_aliases={5: 0, 6: 1},
    )(outer, *even, *odd, acid, left_over)
    return acid[:, None], left_over[:, None]


def solution(mesh):
    sizes = (mesh.shape["depth"], mesh.shape["tx"], mesh.shape["ty"])
    placed = (
        P("tx", "depth", "ty"),
        P("depth", None, None, None),
        P(),
        P(),
        P(),
        P(None, "tx", "depth", "ty"),
    )
    return jax.shard_map(
        functools.partial(on_device, sizes),
        mesh=mesh,
        in_specs=placed,
        out_specs=(P(None, "tx", "depth", "ty"), P(None, "tx", "depth", "ty")),
        check_vma=False,
    )
```
